256 devices in a mesh: patch: 64 (over y, z, x_hi), tensor: 4 (over x_lo, core).
Axes of the slice: x: 4 (x_hi: 2, x_lo: 2; x = x_hi * 2 + x_lo), y: 4, z: 8, core: 2. Of those that a mesh axis runs over, the one named last changes fastest.
Arguments:
- hidden: bfloat16 [8192, 5120], P('patch'), may hold values from -24 to 24
- query: bfloat16 [8192, 2560], P('patch', 'tensor'), may hold values from -16 to 16
- query_gain: float32 [2560], P('tensor'), may hold values from 0.7 to 3.5
- stale_keys: bfloat16 [8192, 2560], P('patch', 'tensor'), may hold values from -192 to 192
- stale_values: bfloat16 [8192, 2560], P('patch', 'tensor'), may hold values from -6 to 6
- out_weight: bfloat16 [2560, 5120], P('tensor'), may hold values from -0.125 to 0.125
- out_bias: float32 [5120], replicated, may hold values from -3 to 3
- residual_gate: float32 [5120], replicated, may hold values from 0.5 to 4
- norm_shift: float32 [5120], replicated, may hold values from -4 to 4
- norm_scale: float32 [5120], replicated, may hold values from -2 to 2
Outputs:
- residual: bfloat16 [8192, 5120], P('patch', 'tensor')
- modulated: bfloat16 [8192, 5120], P('patch', 'tensor')
The draws below stay inside these ranges and needn't reach their ends.
All inputs are finite; a program needn't handle non-finite values.
Results may differ from the reference program's by a relative error of at most 0.0071.
Values may be sent and summed in bfloat16 or wider, within the bound.
A program may use at most 128 MiB of HBM per device.

```python
import math
import jax
import jax.numpy as jnp
from jax import lax

D = 5120
HEAD = 128
HEADS = 20
HD = 2560
TOKENS = 8192


def shared_rows(key):
    return jax.random.truncated_normal(key, -4.0, 4.0, (TOKENS, HD), jnp.float32)


def column_rise(count, lower, upper):
    return jnp.exp(jnp.linspace(math.log(lower), math.log(upper), count)).astype(jnp.float32)


def draw_hidden(key, part):
    key = jax.random.fold_in(key, 7)
    rise = column_rise(D, 0.3, 3.0)
    base = jax.random.truncated_normal(key, -4.0, 4.0, (TOKENS, D), jnp.float32)
    return (base * rise).astype(jnp.bfloat16)


def draw_query(key, part):
    base = shared_rows(key)
    rise = column_rise(HD, 0.5, 2.0)
    return (base * rise).astype(jnp.bfloat16)


def draw_stale_keys(key, part):
    key = jax.random.fold_in(key, 23)
    fresh = jax.random.truncated_normal(key, -4.0, 4.0, (TOKENS, HD), jnp.float32)
    return fresh.astype(jnp.bfloat16)


def levels(rng, extent, shards, low, high):
    level = 1.0
    for position, shards_of in shards:
        draws = jax.random.uniform(jax.random.fold_in(jax.random.fold_in(rng, 6), position), (shards_of,), jnp.float32, low / len(shards), high / len(shards))
        level = level * jnp.repeat(jnp.exp(draws), extent[position] // shards_of).reshape((-1,) + (1,) * (len(extent) - 1 - position))
    return level


def normal_values(key, shape, scale, bound, pieces=(), kind=jnp.bfloat16):
    drawn = scale * jax.random.normal(key, shape, jnp.float32)
    if pieces:
        drawn = drawn * levels(key, shape, pieces, -0.22, 0.18)
    return jnp.clip(drawn, -bound, bound).astype(kind)


def setup_inputs(seed: int = 0) -> dict:
    keys = jax.random.split(jax.random.key(seed), 11)
    return {
        "hidden": draw_hidden(jax.random.fold_in(keys[10], 71), 0),
        "query": draw_query(jax.random.fold_in(keys[10], 71), 0),
        "query_gain": jnp.clip(jnp.exp(math.log(3.5) - 1.609438 * jax.random.uniform(keys[2], (HD,), jnp.float32) ** levels(keys[2], (HD,), ((0, 4),), -0.2, 0.2)), 0.7, 3.5),
        "stale_keys": draw_stale_keys(jax.random.fold_in(keys[10], 71), 0),
        "stale_values": normal_values(keys[4], (TOKENS, HD), 1.0, 6.0, ((0, 64), (1, 4))),
        "out_weight": normal_values(keys[5], (HD, D), HD ** -0.5, 0.125, ((0, 4),)),
        "out_bias": normal_values(keys[6], (D,), 0.5, 3.0, (), jnp.float32),
        "residual_gate": jnp.clip(jnp.exp(jax.random.uniform(keys[7], (D,), jnp.float32, math.log(0.5), math.log(4.0))), 0.5, 4.0),
        "norm_shift": normal_values(keys[8], (D,), 1.0, 4.0, (), jnp.float32),
        "norm_scale": normal_values(keys[9], (D,), 0.5, 2.0, (), jnp.float32),
    }


def attend_block(query_block, keys_wide, values_wide):
    query_wide = query_block.astype(jnp.float32)
    scores = jnp.einsum('bhc,jhc->bhj', query_wide, keys_wide) * HEAD ** (-0.5)
    top = lax.optimization_barrier(jnp.max(scores, axis=2, keepdims=True))
    expo = jnp.exp(scores - top)
    totals = lax.optimization_barrier(jnp.sum(expo, axis=2))
    expo_low = lax.optimization_barrier(expo.astype(jnp.bfloat16)).astype(jnp.float32)
    mixed = jnp.einsum('bhj,jhc->bhc', expo_low, values_wide) / totals[:, :, None]
    return mixed.astype(jnp.bfloat16).reshape(query_block.shape[0], HD)

def reference(hidden, query, query_gain, stale_keys, stale_values, out_weight, out_bias, residual_gate, norm_shift, norm_scale):
    query_wide = query.astype(jnp.float32)
    query_rms = jnp.sqrt(lax.optimization_barrier(jnp.mean(query_wide * query_wide, axis=1)) + 1e-06)
    normed_query = (query_wide / query_rms[:, None] * query_gain).astype(jnp.bfloat16)
    block_rows = math.gcd(TOKENS, 256)
    blocks = normed_query.reshape(TOKENS // block_rows, block_rows, HEADS, HEAD)
    keys_wide = stale_keys.astype(jnp.float32).reshape(TOKENS, HEADS, HEAD)
    values_wide = stale_values.astype(jnp.float32).reshape(TOKENS, HEADS, HEAD)
    attended = lax.map(lambda blk: attend_block(blk, keys_wide, values_wide), blocks).reshape(TOKENS, HD)
    branch = jnp.dot(attended, out_weight, preferred_element_type=jnp.float32) + out_bias
    summed = hidden.astype(jnp.float32) + residual_gate * branch
    row_mean = lax.optimization_barrier(jnp.mean(summed, axis=1))
    row_var = lax.optimization_barrier(jnp.mean(summed * summed, axis=1)) - row_mean * row_mean
    modulated = (summed - row_mean[:, None]) / jnp.sqrt(row_var[:, None] + 1e-06) * (1.0 + norm_scale) + norm_shift
    return (summed.astype(jnp.bfloat16), modulated.astype(jnp.bfloat16))
```

```python
import functools
import math

import jax
import jax.numpy as jnp
from jax import lax
from jax.experimental import pallas as pl
from jax.experimental.pallas import tpu as pltpu
from jax.sharding import PartitionSpec as P

D = 5120
HEAD = 128
HD = 2560
ROWS = 128
NH = 5
NZ = 8
NG = 8
COLS = 1280
PART = 256
NP = COLS // PART
MESH = pl.DeviceIdType.MESH
SCALE = HEAD**-0.5 * math.log2(math.e)


def remote(src, dst, send, recv, device):
    return pltpu.make_async_remote_copy(
        src_ref=src, dst_ref=dst, send_sem=send, recv_sem=recv, device_id=device, device_id_type=MESH
    )


def lanes_of_rows(x):
    ones = jnp.ones((8, x.shape[1]), jnp.float32)
    return lax.dot_general(
        ones, x, (((1,), (1,)), ((), ())), precision=lax.Precision.HIGHEST, preferred_element_type=jnp.float32
    )


def kernel(
    query, gain, keys, values, hidden_hbm, weight_hbm, bias_hbm, gate_hbm, shift_hbm, norm_scale_hbm,
    residual, modulated,
    kbuf, vbuf, qbuf, osend, orecv, ssend, srecv, attended, weight, hidden, params,
    sq, stats, tosib, fromsib, tox, fromx, mine, summed,
    kv_send, kv_recv, q_send, q_recv, o_send, o_recv, s_send, s_recv, sq_send, sq_recv,
    st_send, st_recv, sib_send, sib_recv, x_send, x_recv, local,
):
    patch = lax.axis_index("patch")
    tensor = lax.axis_index("tensor")
    y, z, xh = patch // 16, (patch // 2) % 8, patch % 2
    xl, core = tensor // 2, tensor % 2
    group = y * 2 + xh

    def z_dev(step):
        return {"patch": y * 16 + ((z + step + NZ) % NZ) * 2 + xh, "tensor": tensor}

    def group_dev(r):
        g = (group + r) % NG
        return {"patch": (g // 2) * 16 + z * 2 + g % 2, "tensor": tensor}

    def tensor_dev(r):
        return {"patch": patch, "tensor": (tensor + r) % 4}

    sibling = {"patch": patch, "tensor": xl * 2 + (1 - core)}
    across = {"patch": patch, "tensor": (1 - xl) * 2 + core}

    barrier = pltpu.get_barrier_semaphore()
    for device in [z_dev(1), z_dev(-1)] + [group_dev(r) for r in range(1, NG)] + [tensor_dev(r) for r in range(1, 4)]:
        pl.semaphore_signal(barrier, inc=1, device_id=device, device_id_type=MESH)

    my_cols = pl.ds(pl.multiple_of(tensor * COLS, COLS), COLS)
    local_copies = [pltpu.make_async_copy(weight_hbm, weight, local.at[0])]
    local_copies.append(pltpu.make_async_copy(hidden_hbm.at[:, my_cols], hidden, local.at[1]))
    for i, ref in enumerate((bias_hbm, gate_hbm, shift_hbm, norm_scale_hbm)):
        local_copies.append(pltpu.make_async_copy(ref.at[:, my_cols], params.at[i], local.at[2 + i]))
    for copy in local_copies:
        copy.start()

    for h in range(NH):
        cols = slice(h * HEAD, (h + 1) * HEAD)
        kbuf[h, 0:ROWS, :] = keys[:, cols]
        vbuf[h, :, 0:ROWS] = jnp.transpose(values[:, cols].astype(jnp.float32)).astype(jnp.bfloat16)

    q32 = query[...].astype(jnp.float32)
    sq[0] = lanes_of_rows(q32 * q32)

    pl.semaphore_wait(barrier, 2 + NG - 1 + 3)

    def k_slot(h, d):
        return kbuf.at[h, pl.ds(d * ROWS, ROWS), :]

    def v_slot(h, d):
        return vbuf.at[h, :, pl.ds(d * ROWS, ROWS)]

    def hop(which, h, s, up):
        here = (NZ - s) % NZ if up else s
        there = NZ - s - 1 if up else s + 1
        slot = k_slot if which == 0 else v_slot
        return remote(
            slot(h, here), slot(h, there), kv_send.at[which, int(up), h, s], kv_recv.at[which, h, there],
            z_dev(1 if up else -1),
        )

    def hops(s):
        if s < 3:
            return [(0, True), (1, True), (0, False), (1, False)]
        return [(0, True), (1, False)]

    def arrived(which, h, d):
        slot = k_slot if which == 0 else v_slot
        remote(slot(h, d), slot(h, d), kv_send.at[0, 0, 0, 0], kv_recv.at[which, h, d], z_dev(1)).wait_recv()

    def pass_on(h, s):
        for up in (True, False):
            for which in (0, 1):
                if s > 0:
                    arrived(which, h, NZ - s if up else s)
                if (which, up) in hops(s):
                    hop(which, h, s, up).start()

    pass_on(0, 0)

    def sq_copy(r):
        return remote(sq.at[0], sq.at[4 - r], sq_send.at[r], sq_recv.at[4 - r], tensor_dev(r))

    for r in range(1, 4):
        sq_copy(r).start()
    for h in range(1, NH):
        pass_on(h, 0)
    for r in range(1, 4):
        sq_copy(4 - r).wait_recv()
    squares = sq[0] + sq[1] + sq[2] + sq[3]
    factor = lax.rsqrt(squares / HD + 1e-06) * SCALE
    factor = jnp.transpose(factor)[:, 0:1]
    normed = (q32 * factor * gain[...]).astype(jnp.bfloat16)
    for h in range(NH):
        qbuf[h, 0:ROWS, :] = normed[:, h * HEAD : (h + 1) * HEAD]

    def q_copy(h, r):
        return remote(
            qbuf.at[h, pl.ds(0, ROWS), :], qbuf.at[h, pl.ds((NG - r) * ROWS, ROWS), :],
            q_send.at[h, r], q_recv.at[h, NG - r], group_dev(r),
        )

    def send_queries(h, carry):
        for r in range(1, NG):
            q_copy(h, r).start()
        return carry

    lax.fori_loop(0, NH, send_queries, 0)

    def o_copy(h, r):
        return remote(osend.at[h, r], orecv.at[h, NG - r], o_send.at[h, r], o_recv.at[h, NG - r], group_dev(r))

    def s_copy(h, r):
        return remote(ssend.at[h, r], srecv.at[h, NG - r], s_send.at[h, r], s_recv.at[h, NG - r], group_dev(r))

    def attend(h, j):
        for r in (2 * j, 2 * j + 1):
            if r > 0:
                q_copy(h, NG - r).wait_recv()
        q = qbuf[h, 2 * j * ROWS : (2 * j + 2) * ROWS, :]
        scores = lax.dot_general(kbuf[h], q, (((1,), (1,)), ((), ())), preferred_element_type=jnp.float32)
        top = jnp.max(scores, axis=0, keepdims=True)
        expo = jnp.exp2(scores - top)
        total = jnp.sum(expo, axis=0, keepdims=True)
        mixed = jnp.dot(vbuf[h], expo.astype(jnp.bfloat16), preferred_element_type=jnp.float32)
        for r in (2 * j, 2 * j + 1):
            part = slice((r - 2 * j) * ROWS, (r - 2 * j + 1) * ROWS)
            o_ref, s_ref = (osend, ssend) if r > 0 else (orecv, srecv)
            o_ref[h, r] = mixed[:, part].astype(jnp.bfloat16)
            s_ref[h, r, 0:1, :] = top[:, part]
            s_ref[h, r, 1:2, :] = total[:, part]
            if r > 0:
                o_copy(h, r).start()
                s_copy(h, r).start()

    def combine(h):
        for r in range(1, NG):
            o_copy(h, NG - r).wait_recv()
            s_copy(h, NG - r).wait_recv()
        top = srecv[h, 0, 0:1, :]
        for r in range(1, NG):
            top = jnp.maximum(top, srecv[h, r, 0:1, :])
        num = jnp.zeros((HEAD, ROWS), jnp.float32)
        den = jnp.zeros((1, ROWS), jnp.float32)
        for r in range(NG):
            share = jnp.exp2(srecv[h, r, 0:1, :] - top)
            den = den + share * srecv[h, r, 1:2, :]
            num = num + share * orecv[h, r].astype(jnp.float32)
        attended[:, pl.ds(pl.multiple_of(h * HEAD, HEAD), HEAD)] = jnp.transpose(num / den).astype(jnp.bfloat16)

    def turn(tau, carry):
        for i in range(4):
            if i < 3:
                s = i + 1
                h = tau - i

                @pl.when((h >= 0) & (h < NH))
                def _(h=h, s=s):
                    pass_on(h, s)

            @pl.when((tau >= 3) & (tau < 3 + NH))
            def _(h=tau - 3, i=i):
                if i == 0:
                    arrived(0, h, 4)
                    arrived(1, h, 4)
                attend(h, (i + 1) % 4)

        @pl.when(tau >= 4)
        def _(h=tau - 4):
            combine(h)

        return carry

    lax.fori_loop(0, 4 + NH, turn, 0)

    for copy in local_copies:
        copy.wait()

    def project(block, part):
        cols = pl.ds(pl.multiple_of(block * COLS + part * PART, PART), PART)
        return jnp.dot(attended[...], weight[:, cols], preferred_element_type=jnp.float32)

    def sib_copy(i, part):
        return remote(tosib.at[i, part], fromsib.at[i, part], sib_send.at[i, part], sib_recv.at[i, part], sibling)

    def x_copy(part):
        return remote(tox.at[part], fromx.at[part], x_send.at[part], x_recv.at[part], across)

    def stage(i, block):
        def step(part, carry):
            tosib[i, part] = project(block, part).astype(jnp.bfloat16)
            sib_copy(i, part).start()
            return carry

        lax.fori_loop(0, NP, step, 0)

    stage(0, (1 - xl) * 2 + (1 - core))

    def step_across(part, carry):
        ours = project((1 - xl) * 2 + core, part)
        sib_copy(0, part).wait_recv()
        tox[part] = (ours + fromsib[0, part].astype(jnp.float32)).astype(jnp.bfloat16)
        x_copy(part).start()
        return carry

    lax.fori_loop(0, NP, step_across, 0)
    stage(1, xl * 2 + (1 - core))

    def step_mine(part, carry):
        mine[part] = project(tensor, part)
        return carry

    lax.fori_loop(0, NP, step_mine, 0)

    total = jnp.zeros((ROWS, HEAD), jnp.float32)
    total_sq = jnp.zeros((ROWS, HEAD), jnp.float32)
    for part in range(NP):
        cols = slice(part * PART, (part + 1) * PART)
        sib_copy(1, part).wait_recv()
        x_copy(part).wait_recv()
        branch = mine[part] + fromsib[1, part].astype(jnp.float32) + fromx[part].astype(jnp.float32)
        branch = branch + params[0, :, cols]
        value = hidden[:, cols].astype(jnp.float32) + params[1, :, cols] * branch
        summed[:, cols] = value
        residual[:, cols] = value.astype(jnp.bfloat16)
        for lo in range(0, PART, HEAD):
            piece = value[:, lo : lo + HEAD]
            total = total + piece
            total_sq = total_sq + piece * piece
    stats[0, 0] = lanes_of_rows(total)
    stats[0, 1] = lanes_of_rows(total_sq)

    def st_copy(r):
        return remote(stats.at[0], stats.at[4 - r], st_send.at[r], st_recv.at[4 - r], tensor_dev(r))

    for r in range(1, 4):
        st_copy(r).start()
    for r in range(1, 4):
        st_copy(4 - r).wait_recv()
    mean = (stats[0, 0] + stats[1, 0] + stats[2, 0] + stats[3, 0]) / D
    var = (stats[0, 1] + stats[1, 1] + stats[2, 1] + stats[3, 1]) / D - mean * mean
    inv = lax.rsqrt(var + 1e-06)
    mean = jnp.transpose(mean)[:, 0:1]
    inv = jnp.transpose(inv)[:, 0:1]
    for part in range(NP):
        cols = slice(part * PART, (part + 1) * PART)
        value = (summed[:, cols] - mean) * inv * (1.0 + params[3, :, cols]) + params[2, :, cols]
        modulated[:, cols] = value.astype(jnp.bfloat16)

    def drain(h, carry):
        for s in range(4):
            for which, up in hops(s):
                hop(which, h, s, up).wait_send()
        for r in range(1, NG):
            q_copy(h, r).wait_send()
            o_copy(h, r).wait_send()
            s_copy(h, r).wait_send()
        return carry

    lax.fori_loop(0, NH, drain, 0)
    for r in range(1, 4):
        sq_copy(r).wait_send()
        st_copy(r).wait_send()

    def drain_parts(part, carry):
        sib_copy(0, part).wait_send()
        sib_copy(1, part).wait_send()
        x_copy(part).wait_send()
        return carry

    lax.fori_loop(0, NP, drain_parts, 0)


def body(
    hidden, query, query_gain, stale_keys, stale_values, out_weight, out_bias, residual_gate, norm_shift, norm_scale
):
    bf16, f32 = jnp.bfloat16, jnp.float32
    vmem = pl.BlockSpec(memory_space=pltpu.VMEM)
    hbm = pl.BlockSpec(memory_space=pl.ANY)
    dma = pltpu.SemaphoreType.DMA
    row = lambda x: x.reshape(1, -1)
    out = jax.ShapeDtypeStruct((ROWS, COLS), bf16)
    return pl.pallas_call(
        kernel,
        out_shape=(out, out),
        in_specs=[vmem] * 4 + [hbm] * 6,
        out_specs=(vmem, vmem),
        scratch_shapes=[
            pltpu.VMEM((NH, NZ * ROWS, HEAD), bf16),
            pltpu.VMEM((NH, HEAD, NZ * ROWS), bf16),
            pltpu.VMEM((NH, NG * ROWS, HEAD), bf16),
            pltpu.VMEM((NH, NG, HEAD, ROWS), bf16),
            pltpu.VMEM((NH, NG, HEAD, ROWS), bf16),
            pltpu.VMEM((NH, NG, 8, ROWS), f32),
            pltpu.VMEM((NH, NG, 8, ROWS), f32),
            pltpu.VMEM((ROWS, NH * HEAD), bf16),
            pltpu.VMEM((NH * HEAD, D), bf16),
            pltpu.VMEM((ROWS, COLS), bf16),
            pltpu.VMEM((4, 1, COLS), f32),
            pltpu.VMEM((4, 8, ROWS), f32),
            pltpu.VMEM((4, 2, 8, ROWS), f32),
            pltpu.VMEM((2, NP, ROWS, PART), bf16),
            pltpu.VMEM((2, NP, ROWS, PART), bf16),
            pltpu.VMEM((NP, ROWS, PART), bf16),
            pltpu.VMEM((NP, ROWS, PART), bf16),
            pltpu.VMEM((NP, ROWS, PART), f32),
            pltpu.VMEM((ROWS, COLS), f32),
            dma((2, 2, NH, 4)),
            dma((2, NH, NZ)),
            dma((NH, NG)),
            dma((NH, NG)),
            dma((NH, NG)),
            dma((NH, NG)),
            dma((NH, NG)),
            dma((NH, NG)),
            dma((4,)),
            dma((4,)),
            dma((4,)),
            dma((4,)),
            dma((2, NP)),
            dma((2, NP)),
            dma((NP,)),
            dma((NP,)),
            dma((6,)),
        ],
        compiler_params=pltpu.CompilerParams(
            collective_id=0, has_side_effects=True, vmem_limit_bytes=48 * 2**20
        ),
        name="attention_block",
    )(
        query, row(query_gain), stale_keys, stale_values, hidden, out_weight,
        row(out_bias), row(residual_gate), row(norm_shift), row(norm_scale),
    )


def solution(mesh):
    return jax.shard_map(
        body,
        mesh=mesh,
        in_specs=(
            P("patch", None),
            P("patch", "tensor"),
            P("tensor"),
            P("patch", "tensor"),
            P("patch", "tensor"),
            P("tensor", None),
            P(),
            P(),
            P(),
            P(),
        ),
        out_specs=(P("patch", "tensor"), P("patch", "tensor")),
        check_vma=False,
    )
```

```python
import functools
import math

import jax
import jax.numpy as jnp
from jax import lax
from jax.experimental import pallas as pl
from jax.experimental.pallas import tpu as pltpu
from jax.sharding import PartitionSpec as P

D = 5120
HEAD = 128
HD = 2560
ROWS = 128
NH = 5
GROUPS = ((0, 2), (2, 2), (4, 1))
NG = len(GROUPS)
NZ = 8
NY = 4
NEAR = 5
COLS = 1280
PART = 256
NP = COLS // PART
MESH = pl.DeviceIdType.MESH
SCALE = HEAD**-0.5 * math.log2(math.e)
CONTRACT_LAST = (((1,), (1,)), ((), ()))


def remote(src, dst, send, recv, device):
    return pltpu.make_async_remote_copy(
        src_ref=src, dst_ref=dst, send_sem=send, recv_sem=recv, device_id=device, device_id_type=MESH
    )


def columns_to_rows(first, second):
    n = first.shape[0]
    lane = lax.broadcasted_iota(jnp.int32, (n, HEAD), 1)
    return jnp.transpose(jnp.where(lane == 0, first, second))[0:8]


def kernel(
    query_hbm, gain_hbm, keys_hbm, values_hbm, hidden_hbm, weight_hbm, bias_hbm, gate_hbm, shift_hbm, norm_scale_hbm,
    residual, modulated,
    query, gain, keys, values, weight, hidden, params,
    kvstage, qstage, kv, qbuf, osend, orecv, ssend, srecv, near_mix, near_top, near_total, attended, acc,
    sq, stats, tosib, fromsib, tox, fromx, mine, summed,
    swap_send, kv_send, kv_recv, pair_send, pair_recv, q_send, q_recv, o_send, o_recv, s_send, s_recv, sq_send, sq_recv,
    st_send, st_recv, sib_send, sib_recv, x_send, x_recv, local,
):
    patch = lax.axis_index("patch")
    tensor = lax.axis_index("tensor")
    y, z, xh = patch // 16, (patch // 2) % 8, patch % 2
    xl, core = tensor // 2, tensor % 2
    straight = xh == core

    def z_dev(step):
        return {"patch": y * 16 + ((z + step + NZ) % NZ) * 2 + xh, "tensor": tensor}

    def group_dev(r):
        return {"patch": ((y + r) % NY) * 16 + z * 2 + core, "tensor": xl * 2 + xh}

    def tensor_dev(r):
        return {"patch": patch, "tensor": (tensor + r) % 4}

    sibling = {"patch": patch, "tensor": xl * 2 + (1 - core)}
    across = {"patch": patch, "tensor": (1 - xl) * 2 + core}

    barrier = pltpu.get_barrier_semaphore()
    partners = [z_dev(1), z_dev(-1)] + [group_dev(r) for r in range(1, NY)] + [tensor_dev(r) for r in range(1, 4)]
    for device in partners:
        pl.semaphore_signal(barrier, inc=1, device_id=device, device_id_type=MESH)

    @pl.when(jnp.logical_not(straight))
    def _():
        pl.semaphore_signal(barrier, inc=1, device_id=group_dev(0), device_id_type=MESH)

    my_cols = pl.ds(pl.multiple_of(tensor * COLS, COLS), COLS)
    early = [(keys_hbm, keys), (values_hbm, values), (query_hbm, query), (gain_hbm, gain)]
    late = [(weight_hbm, weight), (hidden_hbm.at[:, my_cols], hidden)]
    late += [(ref.at[:, my_cols], params.at[i]) for i, ref in enumerate((bias_hbm, gate_hbm, shift_hbm, norm_scale_hbm))]
    copies = [pltpu.make_async_copy(src, dst, local.at[i]) for i, (src, dst) in enumerate(early + late)]
    for copy in copies:
        copy.start()

    copies[0].wait()
    copies[1].wait()
    for h in range(NH):
        cols = slice(h * HEAD, (h + 1) * HEAD)
        kvstage[h, 0:ROWS, :] = keys[:, cols]
        kvstage[h, ROWS:, :] = values[:, cols]

    copies[2].wait()
    copies[3].wait()
    q32 = query[...].astype(jnp.float32)
    squares = jnp.sum(q32 * q32, axis=1, keepdims=True)
    sq[0] = columns_to_rows(squares, squares)

    @pl.when(straight)
    def _():
        pl.semaphore_wait(barrier, len(partners))

    @pl.when(jnp.logical_not(straight))
    def _():
        pl.semaphore_wait(barrier, len(partners) + 1)

    def to_group(src, dst, send, recv, r, wait=False):
        copy = remote(src, dst, send, recv, group_dev(r))
        act = copy.wait_send if wait else copy.start
        if r > 0:
            act()
            return
        pl.when(jnp.logical_not(straight))(act)
        if not wait:
            pl.when(straight)(pltpu.make_async_copy(src, dst, recv).start)

    def landed(ref, recv):
        remote(ref, ref, swap_send.at[0], recv, z_dev(1)).wait_recv()

    def heads(g):
        return pl.ds(*GROUPS[g])

    def swap(g, wait=False):
        to_group(kvstage.at[heads(g)], kv.at[0, 0, heads(g)], swap_send.at[g], kv_recv.at[g, 0], 0, wait)

    def place(s, up):
        return 0 if s == 0 else 2 * s - 1 if up or s == 4 else 2 * s

    def block(g, s, up):
        if s == 4:
            return kv.at[7, 0, heads(g), pl.ds(0 if up else ROWS, ROWS)]
        return kv.at[place(s, up), 0, heads(g)]

    def block_sem(g, s, up):
        return kv_recv.at[g, 8 if s == 4 and not up else place(s, up)]

    def hop(g, s, up):
        src = block(g, s, up)
        if s == 3:
            src = kv.at[place(s, up), 0, heads(g), pl.ds(0 if up else ROWS, ROWS)]
        return remote(
            src, block(g, s + 1, up), kv_send.at[g, int(up), s], block_sem(g, s + 1, up), z_dev(1 if up else -1)
        )

    shares = ((0, 1), (1, 2), (3, 2), (5, 3))

    def pair(g, m):
        places = pl.ds(*shares[m])
        return remote(
            kv.at[places, 0, heads(g)], kv.at[places, 1, heads(g)], pair_send.at[g, m], pair_recv.at[g, m], sibling
        )

    def event(g, s):
        if s == 0:
            landed(block(g, 0, True), block_sem(g, 0, True))
        for up in (True, False):
            if s > 0:
                landed(block(g, s, up), block_sem(g, s, up))
            if s < 4:
                hop(g, s, up).start()
        if s != 3:
            pair(g, min(s, 3)).start()

    for g in range(NG):
        swap(g)

    def sq_copy(r):
        return remote(sq.at[0], sq.at[4 - r], sq_send.at[r], sq_recv.at[4 - r], tensor_dev(r))

    for r in range(1, 4):
        sq_copy(r).start()
    event(0, 0)
    event(1, 0)
    for r in range(1, 4):
        sq_copy(4 - r).wait_recv()
    factor = lax.rsqrt((sq[0] + sq[1] + sq[2] + sq[3]) / HD + 1e-06) * SCALE
    factor = jnp.transpose(factor)[:, 0:1]
    normed = (q32 * factor * gain[...][None, :]).astype(jnp.bfloat16)
    for h in range(NH):
        qstage[h] = normed[:, h * HEAD : (h + 1) * HEAD]

    def send_query(r, wait=False):
        back = (NY - r) % NY
        to_group(qstage, qbuf.at[back], q_send.at[r], q_recv.at[back], r, wait)

    for r in range(NY):
        send_query(r)
    event(2, 0)
    event(0, 1)
    event(1, 1)
    for r in range(NY):
        landed(qbuf.at[r], q_recv.at[r])
    event(0, 2)

    def send_mixed(g, r, wait=False):
        back = (NY - r) % NY
        to_group(osend.at[r, heads(g)], orecv.at[back, heads(g)], o_send.at[g, r], o_recv.at[g, back], r, wait)
        to_group(ssend.at[r, heads(g)], srecv.at[back, heads(g)], s_send.at[g, r], s_recv.at[g, back], r, wait)

    def scores_of(h, j, first, count):
        q = qbuf[pl.ds(2 * j, 2), h].reshape(2 * ROWS, HEAD)
        k = kv[first : first + count, :, h, 0:ROWS, :].reshape(count * 2 * ROWS, HEAD)
        return lax.dot_general(q, k, CONTRACT_LAST, preferred_element_type=jnp.float32)

    def mix(h, expo, first, count):
        v = kv[first : first + count, :, h, ROWS : 2 * ROWS, :].reshape(count * 2 * ROWS, HEAD)
        return jnp.dot(expo.astype(jnp.bfloat16), v, preferred_element_type=jnp.float32)

    def attend_near(h, j):
        scores = scores_of(h, j, 0, NEAR)
        top = jnp.max(scores, axis=1, keepdims=True)
        expo = jnp.exp2(scores - top)
        near_top[h, j] = top
        near_total[h, j] = jnp.sum(expo, axis=1, keepdims=True)
        near_mix[h, j] = mix(h, expo, 0, NEAR)

    def attend_far(h, j):
        scores = scores_of(h, j, NEAR, NZ - NEAR)
        top = jnp.maximum(near_top[h, j], jnp.max(scores, axis=1, keepdims=True))
        expo = jnp.exp2(scores - top)
        fade = jnp.exp2(near_top[h, j] - top)
        total = near_total[h, j] * fade + jnp.sum(expo, axis=1, keepdims=True)
        mixed = (near_mix[h, j] * fade + mix(h, expo, NEAR, NZ - NEAR)).astype(jnp.bfloat16)
        numbers = columns_to_rows(top, total)
        for i in range(2):
            part = slice(i * ROWS, (i + 1) * ROWS)
            osend[2 * j + i, h] = mixed[part]
            ssend[2 * j + i, h] = numbers[:, part]

    def near(g, between=None):
        for m in range(3):
            pair(g, m).wait_recv()
        first, count = GROUPS[g]

        def step(i, carry):
            attend_near(first + i % count, 1 - i // count)
            return carry

        lax.fori_loop(0, 2 * count, step, 0)

    def far(g):
        pair(g, 3).wait_recv()
        first, count = GROUPS[g]

        def step(i, carry):
            attend_far(first + i % count, 1 - i // count)
            for j in (1, 0):

                @pl.when(i == (2 - j) * count - 1)
                def _(j=j):
                    send_mixed(g, 2 * j + 1)
                    send_mixed(g, 2 * j)

            return carry

        lax.fori_loop(0, 2 * count, step, 0)

    def combine(g):
        for r in range(NY):
            landed(orecv.at[r, heads(g)], o_recv.at[g, r])
            landed(srecv.at[r, heads(g)], s_recv.at[g, r])
        first, count = GROUPS[g]
        for h in range(first, first + count):
            numbers = jnp.transpose(jnp.concatenate([srecv[r, h] for r in range(NY)], axis=0))
            tops = [numbers[:, 8 * r : 8 * r + 1] for r in range(NY)]
            top = functools.reduce(jnp.maximum, tops)
            shares = [jnp.exp2(t - top) for t in tops]
            den = sum(shares[r] * numbers[:, 8 * r + 1 : 8 * r + 2] for r in range(NY))
            num = sum(shares[r] * orecv[r, h].astype(jnp.float32) for r in range(NY))
            attended[:, h * HEAD : (h + 1) * HEAD] = (num / den).astype(jnp.bfloat16)

    def project(g, columns):
        first, count = GROUPS[g]
        rows = slice(first * HEAD, (first + count) * HEAD)
        return jnp.dot(attended[:, rows], weight[rows, columns], preferred_element_type=jnp.float32)

    def project_early(g):
        def step(b, carry):
            part = project(g, pl.ds(pl.multiple_of(b * COLS, COLS), COLS))
            acc[b] = part if g == 0 else acc[b] + part
            return carry

        lax.fori_loop(0, 4, step, 0)

    event(2, 1)
    event(1, 2)
    near(0)
    event(0, 3)
    event(1, 3)
    event(2, 2)
    event(0, 4)
    near(1)
    event(2, 3)
    event(1, 4)
    far(0)
    near(2)
    event(2, 4)
    far(1)
    copies[4].wait()
    combine(0)
    far(2)
    project_early(0)
    combine(1)
    project_early(1)
    combine(2)

    for copy in copies[5:]:
        copy.wait()

    def branch_part(b, part):
        cols = pl.ds(pl.multiple_of(b * COLS + part * PART, PART), PART)
        return acc[b, :, part * PART : (part + 1) * PART] + project(NG - 1, cols)

    def sib_copy(i, part):
        return remote(tosib.at[i, part], fromsib.at[i, part], sib_send.at[i, part], sib_recv.at[i, part], sibling)

    def x_copy(part):
        return remote(tox.at[part], fromx.at[part], x_send.at[part], x_recv.at[part], across)

    def stage(i, b):
        for part in range(NP):
            tosib[i, part] = branch_part(b, part).astype(jnp.bfloat16)
            sib_copy(i, part).start()

    stage(0, (1 - xl) * 2 + (1 - core))
    for part in range(NP):
        ours = branch_part((1 - xl) * 2 + core, part)
        sib_copy(0, part).wait_recv()
        tox[part] = (ours + fromsib[0, part].astype(jnp.float32)).astype(jnp.bfloat16)
        x_copy(part).start()
    stage(1, xl * 2 + (1 - core))
    for part in range(NP):
        cols = slice(part * PART, (part + 1) * PART)
        branch = branch_part(tensor, part) + params[0, :, cols]
        sib_copy(1, part).wait_recv()
        mine[part] = hidden[:, cols].astype(jnp.float32) + params[1, :, cols] * (
            branch + fromsib[1, part].astype(jnp.float32)
        )

    total = jnp.zeros((ROWS, HEAD), jnp.float32)
    total_sq = jnp.zeros((ROWS, HEAD), jnp.float32)
    for part in range(NP):
        cols = slice(part * PART, (part + 1) * PART)
        x_copy(part).wait_recv()
        value = mine[part] + params[1, :, cols] * fromx[part].astype(jnp.float32)
        summed[:, cols] = value
        residual[:, cols] = value.astype(jnp.bfloat16)
        for lo in range(0, PART, HEAD):
            piece = value[:, lo : lo + HEAD]
            total = total + piece
            total_sq = total_sq + piece * piece
    stats[0] = columns_to_rows(
        jnp.sum(total, axis=1, keepdims=True), jnp.sum(total_sq, axis=1, keepdims=True)
    )

    def st_copy(r):
        return remote(stats.at[0], stats.at[4 - r], st_send.at[r], st_recv.at[4 - r], tensor_dev(r))

    for r in range(1, 4):
        st_copy(r).start()

    for g in range(NG):
        swap(g, wait=True)
        for up in (True, False):
            for s in range(4):
                hop(g, s, up).wait_send()
        for m in range(len(shares)):
            pair(g, m).wait_send()
        for r in range(NY):
            send_mixed(g, r, wait=True)
    for r in range(NY):
        send_query(r, wait=True)
    for r in range(1, 4):
        sq_copy(r).wait_send()
    for part in range(NP):
        sib_copy(0, part).wait_send()
        sib_copy(1, part).wait_send()
        x_copy(part).wait_send()

    for r in range(1, 4):
        st_copy(4 - r).wait_recv()
    both = jnp.transpose(stats[0] + stats[1] + stats[2] + stats[3]) / D
    mean = both[:, 0:1]
    inv = lax.rsqrt(both[:, 1:2] - mean * mean + 1e-06)
    for part in range(NP):
        cols = slice(part * PART, (part + 1) * PART)
        value = (summed[:, cols] - mean) * inv * (1.0 + params[3, :, cols]) + params[2, :, cols]
        modulated[:, cols] = value.astype(jnp.bfloat16)
    for r in range(1, 4):
        st_copy(r).wait_send()


def deliver(first_in, second_in, first_out, second_out, sems):
    half = ROWS // 2
    copies = [
        pltpu.make_async_copy(src.at[pl.ds(i * half, half)], dst.at[pl.ds(i * half, half)], sems.at[2 * k + i])
        for k, (src, dst) in enumerate(((first_in, first_out), (second_in, second_out)))
        for i in range(2)
    ]
    for copy in copies:
        copy.start()
    for copy in copies:
        copy.wait()


def body(
    hidden, query, query_gain, stale_keys, stale_values, out_weight, out_bias, residual_gate, norm_shift, norm_scale
):
    bf16, f32 = jnp.bfloat16, jnp.float32
    vmem = pl.BlockSpec(memory_space=pltpu.VMEM)
    hbm = pl.BlockSpec(memory_space=pltpu.HBM)
    dma = pltpu.SemaphoreType.DMA
    row = lambda x: x.reshape(1, -1)
    out = jax.ShapeDtypeStruct((ROWS, COLS), bf16)
    results = pl.pallas_call(
        kernel,
        out_shape=(out, out),
        in_specs=[hbm] * 10,
        out_specs=(vmem, vmem),
        scratch_shapes=[
            pltpu.VMEM((ROWS, NH * HEAD), bf16),
            pltpu.VMEM((NH * HEAD,), f32),
            pltpu.VMEM((ROWS, NH * HEAD), bf16),
            pltpu.VMEM((ROWS, NH * HEAD), bf16),
            pltpu.VMEM((NH * HEAD, D), bf16),
            pltpu.VMEM((ROWS, COLS), bf16),
            pltpu.VMEM((4, 1, COLS), f32),
            pltpu.VMEM((NH, 2 * ROWS, HEAD), bf16),
            pltpu.VMEM((NH, ROWS, HEAD), bf16),
            pltpu.VMEM((NZ, 2, NH, 2 * ROWS, HEAD), bf16),
            pltpu.VMEM((NY, NH, ROWS, HEAD), bf16),
            pltpu.VMEM((NY, NH, ROWS, HEAD), bf16),
            pltpu.VMEM((NY, NH, ROWS, HEAD), bf16),
            pltpu.VMEM((NY, NH, 8, ROWS), f32),
            pltpu.VMEM((NY, NH, 8, ROWS), f32),
            pltpu.VMEM((NH, 2, 2 * ROWS, HEAD), f32),
            pltpu.VMEM((NH, 2, 2 * ROWS, 1), f32),
            pltpu.VMEM((NH, 2, 2 * ROWS, 1), f32),
            pltpu.VMEM((ROWS, NH * HEAD), bf16),
            pltpu.VMEM((4, ROWS, COLS), f32),
            pltpu.VMEM((4, 8, ROWS), f32),
            pltpu.VMEM((4, 8, ROWS), f32),
            pltpu.VMEM((2, NP, ROWS, PART), bf16),
            pltpu.VMEM((2, NP, ROWS, PART), bf16),
            pltpu.VMEM((NP, ROWS, PART), bf16),
            pltpu.VMEM((NP, ROWS, PART), bf16),
            pltpu.VMEM((NP, ROWS, PART), f32),
            pltpu.VMEM((ROWS, COLS), f32),
            dma((NG,)),
            dma((NG, 2, 4)),
            dma((NG, NZ + 1)),
            dma((NG, 4)),
            dma((NG, 4)),
            dma((NY,)),
            dma((NY,)),
        ]
        + [dma((NG, NY))] * 4
        + [dma((4,))] * 4
        + [dma((2, NP))] * 2
        + [dma((NP,))] * 2
        + [dma((10,))],
        compiler_params=pltpu.CompilerParams(
            collective_id=0, has_side_effects=True, vmem_limit_bytes=56 * 2**20
        ),
        name="attention_block",
    )(
        query, query_gain, stale_keys, stale_values, hidden, out_weight,
        row(out_bias), row(residual_gate), row(norm_shift), row(norm_scale),
    )
    return pl.pallas_call(
        deliver,
        out_shape=(out, out),
        in_specs=[hbm] * 2,
        out_specs=(hbm, hbm),
        scratch_shapes=[dma((4,))],
        name="deliver",
    )(*results)


def solution(mesh):
    return jax.shard_map(
        body,
        mesh=mesh,
        in_specs=(
            P("patch", None),
            P("patch", "tensor"),
            P("tensor"),
            P("patch", "tensor"),
            P("patch", "tensor"),
            P("tensor", None),
            P(),
            P(),
            P(),
            P(),
        ),
        out_specs=(P("patch", "tensor"), P("patch", "tensor")),
        check_vma=False,
    )
```

```python
import functools
import math

import jax
import jax.numpy as jnp
from jax import lax
from jax.experimental import pallas as pl
from jax.experimental.pallas import tpu as pltpu
from jax.sharding import PartitionSpec as P

D = 5120
HEAD = 128
HD = 2560
ROWS = 128
NH = 5
GROUPS = ((0, 1), (1, 2), (3, 1), (4, 1))
NG = len(GROUPS)
NZ = 8
NY = 4
NEAR = 5
COLS = 1280
PART = 256
NP = COLS // PART
MESH = pl.DeviceIdType.MESH
SCALE = HEAD**-0.5 * math.log2(math.e)
CONTRACT_LAST = (((1,), (1,)), ((), ()))


def remote(src, dst, send, recv, device):
    return pltpu.make_async_remote_copy(
        src_ref=src, dst_ref=dst, send_sem=send, recv_sem=recv, device_id=device, device_id_type=MESH
    )


def columns_to_rows(first, second):
    n = first.shape[0]
    lane = lax.broadcasted_iota(jnp.int32, (n, HEAD), 1)
    return jnp.transpose(jnp.where(lane == 0, first, second))[0:8]


def kernel(
    query_hbm, gain_hbm, keys_hbm, values_hbm, hidden_hbm, weight_hbm, bias_hbm, gate_hbm, shift_hbm, norm_scale_hbm,
    residual, modulated,
    query, gain, keys, values, weight, hidden, params,
    kvstage, qstage, kv, qbuf, osend, orecv, ssend, srecv, near_mix, near_top, near_total, attended, acc,
    sq, stats, tosib, fromsib, tox, fromx, mine, summed,
    swap_send, kv_send, kv_recv, pair_send, pair_recv, q_send, q_recv, o_send, o_recv, s_send, s_recv, sq_send, sq_recv,
    st_send, st_recv, sib_send, sib_recv, x_send, x_recv, local,
):
    patch = lax.axis_index("patch")
    tensor = lax.axis_index("tensor")
    y, z, xh = patch // 16, (patch // 2) % 8, patch % 2
    xl, core = tensor // 2, tensor % 2
    straight = xh == core

    def z_dev(step):
        return {"patch": y * 16 + ((z + step + NZ) % NZ) * 2 + xh, "tensor": tensor}

    def group_dev(r):
        return {"patch": ((y + r) % NY) * 16 + z * 2 + core, "tensor": xl * 2 + xh}

    def tensor_dev(r):
        return {"patch": patch, "tensor": (tensor + r) % 4}

    sibling = {"patch": patch, "tensor": xl * 2 + (1 - core)}
    across = {"patch": patch, "tensor": (1 - xl) * 2 + core}

    barrier = pltpu.get_barrier_semaphore()
    partners = [z_dev(1), z_dev(-1)] + [group_dev(r) for r in range(1, NY)] + [tensor_dev(r) for r in range(1, 4)]
    for device in partners:
        pl.semaphore_signal(barrier, inc=1, device_id=device, device_id_type=MESH)

    @pl.when(jnp.logical_not(straight))
    def _():
        pl.semaphore_signal(barrier, inc=1, device_id=group_dev(0), device_id_type=MESH)

    my_cols = pl.ds(pl.multiple_of(tensor * COLS, COLS), COLS)
    early = [(keys_hbm, keys), (values_hbm, values), (query_hbm, query), (gain_hbm, gain)]
    late = [(weight_hbm, weight), (hidden_hbm.at[:, my_cols], hidden)]
    late += [(ref.at[:, my_cols], params.at[i]) for i, ref in enumerate((bias_hbm, gate_hbm, shift_hbm, norm_scale_hbm))]
    copies = [pltpu.make_async_copy(src, dst, local.at[i]) for i, (src, dst) in enumerate(early + late)]
    for copy in copies:
        copy.start()

    copies[0].wait()
    copies[1].wait()
    for h in range(NH):
        cols = slice(h * HEAD, (h + 1) * HEAD)
        kvstage[h, 0:ROWS, :] = keys[:, cols]
        kvstage[h, ROWS:, :] = values[:, cols]

    copies[2].wait()
    copies[3].wait()
    q32 = query[...].astype(jnp.float32)
    squares = jnp.sum(q32 * q32, axis=1, keepdims=True)
    sq[0] = columns_to_rows(squares, squares)

    @pl.when(straight)
    def _():
        pl.semaphore_wait(barrier, len(partners))

    @pl.when(jnp.logical_not(straight))
    def _():
        pl.semaphore_wait(barrier, len(partners) + 1)

    def to_group(src, dst, send, recv, r, wait=False):
        copy = remote(src, dst, send, recv, group_dev(r))
        act = copy.wait_send if wait else copy.start
        if r > 0:
            act()
            return
        pl.when(jnp.logical_not(straight))(act)
        if not wait:
            pl.when(straight)(pltpu.make_async_copy(src, dst, recv).start)

    def landed(ref, recv):
        remote(ref, ref, swap_send.at[0], recv, z_dev(1)).wait_recv()

    def heads(g):
        return pl.ds(*GROUPS[g])

    def swap(g, wait=False):
        to_group(kvstage.at[heads(g)], kv.at[0, 0, heads(g)], swap_send.at[g], kv_recv.at[g, 0], 0, wait)

    def place(s, up):
        return 0 if s == 0 else 2 * s - 1 if up or s == 4 else 2 * s

    def block(g, s, up):
        if s == 4:
            return kv.at[7, 0, heads(g), pl.ds(0 if up else ROWS, ROWS)]
        return kv.at[place(s, up), 0, heads(g)]

    def block_sem(g, s, up):
        return kv_recv.at[g, 8 if s == 4 and not up else place(s, up)]

    def hop(g, s, up):
        src = block(g, s, up)
        if s == 3:
            src = kv.at[place(s, up), 0, heads(g), pl.ds(0 if up else ROWS, ROWS)]
        return remote(
            src, block(g, s + 1, up), kv_send.at[g, int(up), s], block_sem(g, s + 1, up), z_dev(1 if up else -1)
        )

    shares = ((0, 1), (1, 2), (3, 2), (5, 3))

    def pair(g, m):
        places = pl.ds(*shares[m])
        return remote(
            kv.at[places, 0, heads(g)], kv.at[places, 1, heads(g)], pair_send.at[g, m], pair_recv.at[g, m], sibling
        )

    def event(g, s):
        if s == 0:
            landed(block(g, 0, True), block_sem(g, 0, True))
        for up in (True, False):
            if s > 0:
                landed(block(g, s, up), block_sem(g, s, up))
            if s < 4:
                hop(g, s, up).start()
        if s != 3:
            pair(g, min(s, 3)).start()

    swap(0)
    swap(1)

    def sq_copy(r):
        return remote(sq.at[0], sq.at[4 - r], sq_send.at[r], sq_recv.at[4 - r], tensor_dev(r))

    for r in range(1, 4):
        sq_copy(r).start()
    event(0, 0)
    swap(2)
    event(1, 0)
    swap(3)
    for r in range(1, 4):
        sq_copy(4 - r).wait_recv()
    factor = lax.rsqrt((sq[0] + sq[1] + sq[2] + sq[3]) / HD + 1e-06) * SCALE
    factor = jnp.transpose(factor)[:, 0:1]
    normed = (q32 * factor * gain[...][None, :]).astype(jnp.bfloat16)
    for h in range(NH):
        qstage[h] = normed[:, h * HEAD : (h + 1) * HEAD]

    def send_query(r, wait=False):
        back = (NY - r) % NY
        to_group(qstage, qbuf.at[back], q_send.at[r], q_recv.at[back], r, wait)

    for r in range(NY):
        send_query(r)
    event(0, 1)
    event(2, 0)
    event(1, 1)
    event(0, 2)
    event(3, 0)
    event(2, 1)
    for r in range(NY):
        landed(qbuf.at[r], q_recv.at[r])

    def send_mixed(g, r, wait=False):
        back = (NY - r) % NY
        to_group(osend.at[r, heads(g)], orecv.at[back, heads(g)], o_send.at[g, r], o_recv.at[g, back], r, wait)
        to_group(ssend.at[r, heads(g)], srecv.at[back, heads(g)], s_send.at[g, r], s_recv.at[g, back], r, wait)

    def scores_of(h, j, first, count):
        q = qbuf[pl.ds(2 * j, 2), h].reshape(2 * ROWS, HEAD)
        k = kv[first : first + count, :, h, 0:ROWS, :].reshape(count * 2 * ROWS, HEAD)
        return lax.dot_general(q, k, CONTRACT_LAST, preferred_element_type=jnp.float32)

    def mix(h, expo, first, count):
        v = kv[first : first + count, :, h, ROWS : 2 * ROWS, :].reshape(count * 2 * ROWS, HEAD)
        return jnp.dot(expo.astype(jnp.bfloat16), v, preferred_element_type=jnp.float32)

    def attend_near(h, j):
        scores = scores_of(h, j, 0, NEAR)
        top = jnp.max(scores, axis=1, keepdims=True)
        expo = jnp.exp2(scores - top)
        near_top[h, j] = top
        near_total[h, j] = jnp.sum(expo, axis=1, keepdims=True)
        near_mix[h, j] = mix(h, expo, 0, NEAR)

    def attend_far(h, j):
        scores = scores_of(h, j, NEAR, NZ - NEAR)
        top = jnp.maximum(near_top[h, j], jnp.max(scores, axis=1, keepdims=True))
        expo = jnp.exp2(scores - top)
        fade = jnp.exp2(near_top[h, j] - top)
        total = near_total[h, j] * fade + jnp.sum(expo, axis=1, keepdims=True)
        mixed = (near_mix[h, j] * fade + mix(h, expo, NEAR, NZ - NEAR)).astype(jnp.bfloat16)
        numbers = columns_to_rows(top, total)
        for i in range(2):
            part = slice(i * ROWS, (i + 1) * ROWS)
            osend[2 * j + i, h] = mixed[part]
            ssend[2 * j + i, h] = numbers[:, part]

    def near(g, between=None):
        for m in range(3):
            pair(g, m).wait_recv()
        first, count = GROUPS[g]

        def step(i, carry):
            attend_near(first + i % count, 1 - i // count)
            return carry

        lax.fori_loop(0, 2 * count, step, 0)

    def far(g):
        pair(g, 3).wait_recv()
        first, count = GROUPS[g]

        def step(i, carry):
            attend_far(first + i % count, 1 - i // count)
            for j in (1, 0):

                @pl.when(i == (2 - j) * count - 1)
                def _(j=j):
                    send_mixed(g, 2 * j + 1)
                    send_mixed(g, 2 * j)

            return carry

        lax.fori_loop(0, 2 * count, step, 0)

    def combine(g):
        for r in range(NY):
            landed(orecv.at[r, heads(g)], o_recv.at[g, r])
            landed(srecv.at[r, heads(g)], s_recv.at[g, r])
        first, count = GROUPS[g]
        for h in range(first, first + count):
            numbers = jnp.transpose(jnp.concatenate([srecv[r, h] for r in range(NY)], axis=0))
            tops = [numbers[:, 8 * r : 8 * r + 1] for r in range(NY)]
            top = functools.reduce(jnp.maximum, tops)
            shares = [jnp.exp2(t - top) for t in tops]
            den = sum(shares[r] * numbers[:, 8 * r + 1 : 8 * r + 2] for r in range(NY))
            num = sum(shares[r] * orecv[r, h].astype(jnp.float32) for r in range(NY))
            attended[:, h * HEAD : (h + 1) * HEAD] = (num / den).astype(jnp.bfloat16)

    def project(first, count, columns):
        rows = slice(first * HEAD, (first + count) * HEAD)
        return jnp.dot(attended[:, rows], weight[rows, columns], preferred_element_type=jnp.float32)

    def project_early():
        def step(b, carry):
            acc[b] = project(0, NH - 1, pl.ds(pl.multiple_of(b * COLS, COLS), COLS))
            return carry

        lax.fori_loop(0, 4, step, 0)

    near(0)
    event(1, 2)
    event(0, 3)
    near(1)
    event(3, 1)
    event(2, 2)
    event(0, 4)
    event(1, 3)
    near(2)
    far(0)
    event(3, 2)
    event(2, 3)
    near(3)
    event(1, 4)
    copies[4].wait()
    combine(0)
    event(3, 3)
    event(2, 4)
    far(1)
    event(3, 4)
    far(2)
    far(3)
    combine(1)
    combine(2)
    project_early()
    combine(3)

    for copy in copies[5:]:
        copy.wait()

    def branch_part(b, part):
        cols = pl.ds(pl.multiple_of(b * COLS + part * PART, PART), PART)
        return acc[b, :, part * PART : (part + 1) * PART] + project(NH - 1, 1, cols)

    def sib_copy(i, part):
        return remote(tosib.at[i, part], fromsib.at[i, part], sib_send.at[i, part], sib_recv.at[i, part], sibling)

    def x_copy(part):
        return remote(tox.at[part], fromx.at[part], x_send.at[part], x_recv.at[part], across)

    def stage(i, b):
        for part in range(NP):
            tosib[i, part] = branch_part(b, part).astype(jnp.bfloat16)
            sib_copy(i, part).start()

    stage(0, (1 - xl) * 2 + (1 - core))
    for part in range(NP):
        ours = branch_part((1 - xl) * 2 + core, part)
        sib_copy(0, part).wait_recv()
        tox[part] = (ours + fromsib[0, part].astype(jnp.float32)).astype(jnp.bfloat16)
        x_copy(part).start()
    stage(1, xl * 2 + (1 - core))
    for part in range(NP):
        cols = slice(part * PART, (part + 1) * PART)
        branch = branch_part(tensor, part) + params[0, :, cols]
        sib_copy(1, part).wait_recv()
        mine[part] = hidden[:, cols].astype(jnp.float32) + params[1, :, cols] * (
            branch + fromsib[1, part].astype(jnp.float32)
        )

    total = jnp.zeros((ROWS, HEAD), jnp.float32)
    total_sq = jnp.zeros((ROWS, HEAD), jnp.float32)
    for part in range(NP):
        cols = slice(part * PART, (part + 1) * PART)
        x_copy(part).wait_recv()
        value = mine[part] + params[1, :, cols] * fromx[part].astype(jnp.float32)
        summed[:, cols] = value
        residual[:, cols] = value.astype(jnp.bfloat16)
        for lo in range(0, PART, HEAD):
            piece = value[:, lo : lo + HEAD]
            total = total + piece
            total_sq = total_sq + piece * piece
    stats[0] = columns_to_rows(
        jnp.sum(total, axis=1, keepdims=True), jnp.sum(total_sq, axis=1, keepdims=True)
    )

    def st_copy(r):
        return remote(stats.at[0], stats.at[4 - r], st_send.at[r], st_recv.at[4 - r], tensor_dev(r))

    for r in range(1, 4):
        st_copy(r).start()

    for g in range(NG):
        swap(g, wait=True)
        for up in (True, False):
            for s in range(4):
                hop(g, s, up).wait_send()
        for m in range(len(shares)):
            pair(g, m).wait_send()
        for r in range(NY):
            send_mixed(g, r, wait=True)
    for r in range(NY):
        send_query(r, wait=True)
    for r in range(1, 4):
        sq_copy(r).wait_send()
    for part in range(NP):
        sib_copy(0, part).wait_send()
        sib_copy(1, part).wait_send()
        x_copy(part).wait_send()

    for r in range(1, 4):
        st_copy(4 - r).wait_recv()
    both = jnp.transpose(stats[0] + stats[1] + stats[2] + stats[3]) / D
    mean = both[:, 0:1]
    inv = lax.rsqrt(both[:, 1:2] - mean * mean + 1e-06)
    for part in range(NP):
        cols = slice(part * PART, (part + 1) * PART)
        value = (summed[:, cols] - mean) * inv * (1.0 + params[3, :, cols]) + params[2, :, cols]
        modulated[:, cols] = value.astype(jnp.bfloat16)
    for r in range(1, 4):
        st_copy(r).wait_send()


def deliver(first_in, second_in, first_out, second_out):
    first_out[...] = first_in[...]
    second_out[...] = second_in[...]


def body(
    hidden, query, query_gain, stale_keys, stale_values, out_weight, out_bias, residual_gate, norm_shift, norm_scale
):
    bf16, f32 = jnp.bfloat16, jnp.float32
    vmem = pl.BlockSpec(memory_space=pltpu.VMEM)
    hbm = pl.BlockSpec(memory_space=pltpu.HBM)
    dma = pltpu.SemaphoreType.DMA
    row = lambda x: x.reshape(1, -1)
    out = jax.ShapeDtypeStruct((ROWS, COLS), bf16)
    results = pl.pallas_call(
        kernel,
        out_shape=(out, out),
        in_specs=[hbm] * 10,
        out_specs=(vmem, vmem),
        scratch_shapes=[
            pltpu.VMEM((ROWS, NH * HEAD), bf16),
            pltpu.VMEM((NH * HEAD,), f32),
            pltpu.VMEM((ROWS, NH * HEAD), bf16),
            pltpu.VMEM((ROWS, NH * HEAD), bf16),
            pltpu.VMEM((NH * HEAD, D), bf16),
            pltpu.VMEM((ROWS, COLS), bf16),
            pltpu.VMEM((4, 1, COLS), f32),
            pltpu.VMEM((NH, 2 * ROWS, HEAD), bf16),
            pltpu.VMEM((NH, ROWS, HEAD), bf16),
            pltpu.VMEM((NZ, 2, NH, 2 * ROWS, HEAD), bf16),
            pltpu.VMEM((NY, NH, ROWS, HEAD), bf16),
            pltpu.VMEM((NY, NH, ROWS, HEAD), bf16),
            pltpu.VMEM((NY, NH, ROWS, HEAD), bf16),
            pltpu.VMEM((NY, NH, 8, ROWS), f32),
            pltpu.VMEM((NY, NH, 8, ROWS), f32),
            pltpu.VMEM((NH, 2, 2 * ROWS, HEAD), f32),
            pltpu.VMEM((NH, 2, 2 * ROWS, 1), f32),
            pltpu.VMEM((NH, 2, 2 * ROWS, 1), f32),
            pltpu.VMEM((ROWS, NH * HEAD), bf16),
            pltpu.VMEM((4, ROWS, COLS), f32),
            pltpu.VMEM((4, 8, ROWS), f32),
            pltpu.VMEM((4, 8, ROWS), f32),
            pltpu.VMEM((2, NP, ROWS, PART), bf16),
            pltpu.VMEM((2, NP, ROWS, PART), bf16),
            pltpu.VMEM((NP, ROWS, PART), bf16),
            pltpu.VMEM((NP, ROWS, PART), bf16),
            pltpu.VMEM((NP, ROWS, PART), f32),
            pltpu.VMEM((ROWS, COLS), f32),
            dma((NG,)),
            dma((NG, 2, 4)),
            dma((NG, NZ + 1)),
            dma((NG, 4)),
            dma((NG, 4)),
            dma((NY,)),
            dma((NY,)),
        ]
        + [dma((NG, NY))] * 4
        + [dma((4,))] * 4
        + [dma((2, NP))] * 2
        + [dma((NP,))] * 2
        + [dma((10,))],
        compiler_params=pltpu.CompilerParams(
            collective_id=0, has_side_effects=True, vmem_limit_bytes=56 * 2**20
        ),
        name="attention_block",
    )(
        query, query_gain, stale_keys, stale_values, hidden, out_weight,
        row(out_bias), row(residual_gate), row(norm_shift), row(norm_scale),
    )
    return pl.pallas_call(
        deliver,
        out_shape=(out, out),
        in_specs=[vmem] * 2,
        out_specs=(vmem, vmem),
        compiler_params=pltpu.CompilerParams(vmem_limit_bytes=56 * 2**20),
        name="deliver",
    )(*results)


def solution(mesh):
    return jax.shard_map(
        body,
        mesh=mesh,
        in_specs=(
            P("patch", None),
            P("patch", "tensor"),
            P("tensor"),
            P("patch", "tensor"),
            P("patch", "tensor"),
            P("tensor", None),
            P(),
            P(),
            P(),
            P(),
        ),
        out_specs=(P("patch", "tensor"), P("patch", "tensor")),
        check_vma=False,
    )
```

```python
import functools
import math

import jax
import jax.numpy as jnp
from jax import lax
from jax.experimental import pallas as pl
from jax.experimental.pallas import tpu as pltpu
from jax.sharding import PartitionSpec as P

D = 5120
HEAD = 128
HD = 2560
ROWS = 128
NH = 5
GROUPS = ((0, 1), (1, 2), (3, 1), (4, 1))
NG = len(GROUPS)
NZ = 8
NY = 4
NEAR = 5
COLS = 1280
PART = 256
NP = COLS // PART
MESH = pl.DeviceIdType.MESH
SCALE = HEAD**-0.5 * math.log2(math.e)
CONTRACT_LAST = (((1,), (1,)), ((), ()))


def remote(src, dst, send, recv, device):
    return pltpu.make_async_remote_copy(
        src_ref=src, dst_ref=dst, send_sem=send, recv_sem=recv, device_id=device, device_id_type=MESH
    )


def columns_to_rows(first, second):
    n = first.shape[0]
    lane = lax.broadcasted_iota(jnp.int32, (n, HEAD), 1)
    return jnp.transpose(jnp.where(lane == 0, first, second))[0:8]


def kernel(
    query_hbm, gain_hbm, keys_hbm, values_hbm, hidden_hbm, weight_hbm, bias_hbm, gate_hbm, shift_hbm, norm_scale_hbm,
    residual, modulated,
    query, gain, keys, values, weight, hidden, params,
    kvstage, qstage, kv, qbuf, osend, orecv, ssend, srecv, near_mix, near_top, near_total, attended, acc,
    sq, stats, tosib, fromsib, tox, fromx, mine, summed,
    swap_send, kv_send, kv_recv, pair_send, pair_recv, q_send, q_recv, o_send, o_recv, s_send, s_recv, sq_send, sq_recv,
    st_send, st_recv, sib_send, sib_recv, x_send, x_recv, local,
):
    patch = lax.axis_index("patch")
    tensor = lax.axis_index("tensor")
    y, z, xh = patch // 16, (patch // 2) % 8, patch % 2
    xl, core = tensor // 2, tensor % 2
    straight = xh == core

    def z_dev(step):
        return {"patch": y * 16 + ((z + step + NZ) % NZ) * 2 + xh, "tensor": tensor}

    def group_dev(r):
        return {"patch": ((y + r) % NY) * 16 + z * 2 + core, "tensor": xl * 2 + xh}

    def tensor_dev(r):
        return {"patch": patch, "tensor": (tensor + r) % 4}

    sibling = {"patch": patch, "tensor": xl * 2 + (1 - core)}
    across = {"patch": patch, "tensor": (1 - xl) * 2 + core}

    barrier = pltpu.get_barrier_semaphore()
    partners = [z_dev(1), z_dev(-1)] + [group_dev(r) for r in range(1, NY)] + [tensor_dev(r) for r in range(1, 4)]
    for device in partners:
        pl.semaphore_signal(barrier, inc=1, device_id=device, device_id_type=MESH)

    @pl.when(jnp.logical_not(straight))
    def _():
        pl.semaphore_signal(barrier, inc=1, device_id=group_dev(0), device_id_type=MESH)

    my_cols = pl.ds(pl.multiple_of(tensor * COLS, COLS), COLS)
    early = [(keys_hbm, keys), (values_hbm, values), (query_hbm, query), (gain_hbm, gain)]
    late = [(weight_hbm, weight), (hidden_hbm.at[:, my_cols], hidden)]
    late += [(ref.at[:, my_cols], params.at[i]) for i, ref in enumerate((bias_hbm, gate_hbm, shift_hbm, norm_scale_hbm))]
    copies = [pltpu.make_async_copy(src, dst, local.at[i]) for i, (src, dst) in enumerate(early + late)]
    for copy in copies:
        copy.start()

    copies[0].wait()
    copies[1].wait()
    for h in range(NH):
        cols = slice(h * HEAD, (h + 1) * HEAD)
        kvstage[h, 0:ROWS, :] = keys[:, cols]
        kvstage[h, ROWS:, :] = values[:, cols]

    copies[2].wait()
    copies[3].wait()
    q32 = query[...].astype(jnp.float32)
    squares = jnp.sum(q32 * q32, axis=1, keepdims=True)
    sq[0] = columns_to_rows(squares, squares)

    @pl.when(straight)
    def _():
        pl.semaphore_wait(barrier, len(partners))

    @pl.when(jnp.logical_not(straight))
    def _():
        pl.semaphore_wait(barrier, len(partners) + 1)

    def to_group(src, dst, send, recv, r, wait=False):
        copy = remote(src, dst, send, recv, group_dev(r))
        act = copy.wait_send if wait else copy.start
        if r > 0:
            act()
            return
        pl.when(jnp.logical_not(straight))(act)
        if not wait:

            @pl.when(straight)
            def _():
                dst[...] = src[...]

    def landed(ref, recv, r=1):
        wait = remote(ref, ref, swap_send.at[0], recv, z_dev(1)).wait_recv
        if r > 0:
            wait()
        else:
            pl.when(jnp.logical_not(straight))(wait)

    def heads(g):
        return pl.ds(*GROUPS[g])

    def swap(g, wait=False):
        to_group(kvstage.at[heads(g)], kv.at[0, 0, heads(g)], swap_send.at[g], kv_recv.at[g, 0], 0, wait)

    def place(s, up):
        return 0 if s == 0 else 2 * s - 1 if up or s == 4 else 2 * s

    def block(g, s, up):
        if s == 4:
            return kv.at[7, 0, heads(g), pl.ds(0 if up else ROWS, ROWS)]
        return kv.at[place(s, up), 0, heads(g)]

    def block_sem(g, s, up):
        return kv_recv.at[g, 8 if s == 4 and not up else place(s, up)]

    def hop(g, s, up):
        src = block(g, s, up)
        if s == 3:
            src = kv.at[place(s, up), 0, heads(g), pl.ds(0 if up else ROWS, ROWS)]
        return remote(
            src, block(g, s + 1, up), kv_send.at[g, int(up), s], block_sem(g, s + 1, up), z_dev(1 if up else -1)
        )

    shares = ((0, 1), (1, 2), (3, 2), (5, 3))

    def pair(g, m):
        places = pl.ds(*shares[m])
        return remote(
            kv.at[places, 0, heads(g)], kv.at[places, 1, heads(g)], pair_send.at[g, m], pair_recv.at[g, m], sibling
        )

    def event(g, s):
        if s == 0:
            landed(block(g, 0, True), block_sem(g, 0, True), 0)
        for up in (True, False):
            if s > 0:
                landed(block(g, s, up), block_sem(g, s, up))
            if s < 4:
                hop(g, s, up).start()
        if s != 3:
            pair(g, min(s, 3)).start()

    for g in range(min(2, NG)):
        swap(g)

    def sq_copy(r):
        return remote(sq.at[0], sq.at[4 - r], sq_send.at[r], sq_recv.at[4 - r], tensor_dev(r))

    for r in range(1, 4):
        sq_copy(r).start()
    event(0, 0)
    swap(2)
    event(1, 0)
    swap(3)
    for r in range(1, 4):
        sq_copy(4 - r).wait_recv()
    factor = lax.rsqrt((sq[0] + sq[1] + sq[2] + sq[3]) / HD + 1e-06) * SCALE
    factor = jnp.transpose(factor)[:, 0:1]
    normed = (q32 * factor * gain[...][None, :]).astype(jnp.bfloat16)
    for h in range(NH):
        qstage[h] = normed[:, h * HEAD : (h + 1) * HEAD]

    def send_query(r, wait=False):
        back = (NY - r) % NY
        to_group(qstage, qbuf.at[back], q_send.at[r], q_recv.at[back], r, wait)

    for r in range(NY):
        send_query(r)
    event(2, 0)
    event(3, 0)

    def send_mixed(g, r, wait=False):
        back = (NY - r) % NY
        to_group(osend.at[r, heads(g)], orecv.at[back, heads(g)], o_send.at[g, r], o_recv.at[g, back], r, wait)
        to_group(ssend.at[r, heads(g)], srecv.at[back, heads(g)], s_send.at[g, r], s_recv.at[g, back], r, wait)

    def scores_of(h, j, first, count):
        q = qbuf[pl.ds(2 * j, 2), h].reshape(2 * ROWS, HEAD)
        k = kv[first : first + count, :, h, 0:ROWS, :].reshape(count * 2 * ROWS, HEAD)
        return lax.dot_general(q, k, CONTRACT_LAST, preferred_element_type=jnp.float32)

    def mix(h, expo, first, count):
        v = kv[first : first + count, :, h, ROWS : 2 * ROWS, :].reshape(count * 2 * ROWS, HEAD)
        return jnp.dot(expo.astype(jnp.bfloat16), v, preferred_element_type=jnp.float32)

    def attend_near(h, j):
        scores = scores_of(h, j, 0, NEAR)
        top = jnp.max(scores, axis=1, keepdims=True)
        expo = jnp.exp2(scores - top)
        near_top[h, j] = top
        near_total[h, j] = jnp.sum(expo, axis=1, keepdims=True)
        near_mix[h, j] = mix(h, expo, 0, NEAR)

    def attend_far(h, j):
        scores = scores_of(h, j, NEAR, NZ - NEAR)
        top = jnp.maximum(near_top[h, j], jnp.max(scores, axis=1, keepdims=True))
        expo = jnp.exp2(scores - top)
        fade = jnp.exp2(near_top[h, j] - top)
        total = near_total[h, j] * fade + jnp.sum(expo, axis=1, keepdims=True)
        mixed = (near_mix[h, j] * fade + mix(h, expo, NEAR, NZ - NEAR)).astype(jnp.bfloat16)
        numbers = columns_to_rows(top, total)
        for i in range(2):
            part = slice(i * ROWS, (i + 1) * ROWS)
            osend[2 * j + i, h] = mixed[part]
            ssend[2 * j + i, h] = numbers[:, part]

    def near(g, start, stop):
        if start == 0:
            for m in range(3):
                pair(g, m).wait_recv()
        first, count = GROUPS[g]

        def step(i, carry):
            attend_near(first + i % count, 1 - i // count)
            return carry

        lax.fori_loop(start, stop, step, 0)

    def far(g, start, stop):
        if start == 0:
            pair(g, 3).wait_recv()
        first, count = GROUPS[g]

        def step(i, carry):
            attend_far(first + i % count, 1 - i // count)
            for j in (1, 0):

                @pl.when(i == (2 - j) * count - 1)
                def _(j=j):
                    send_mixed(g, 2 * j + 1)
                    send_mixed(g, 2 * j)

            return carry

        lax.fori_loop(start, stop, step, 0)

    def combine(g):
        for r in range(NY):
            landed(orecv.at[r, heads(g)], o_recv.at[g, r], r)
            landed(srecv.at[r, heads(g)], s_recv.at[g, r], r)
        first, count = GROUPS[g]
        for h in range(first, first + count):
            tops = [srecv[r, h, 0:1, :] for r in range(NY)]
            top = functools.reduce(jnp.maximum, tops)
            shares = [jnp.exp2(t - top) for t in tops]
            den = sum(shares[r] * srecv[r, h, 1:2, :] for r in range(NY))
            scales = jnp.transpose(jnp.concatenate([share / den for share in shares] * 2, axis=0))
            num = sum(scales[:, r : r + 1] * orecv[r, h].astype(jnp.float32) for r in range(NY))
            attended[:, h * HEAD : (h + 1) * HEAD] = num.astype(jnp.bfloat16)

    def project(first, count, columns):
        rows = slice(first * HEAD, (first + count) * HEAD)
        return jnp.dot(attended[:, rows], weight[rows, columns], preferred_element_type=jnp.float32)

    def project_early():
        def step(b, carry):
            acc[b] = project(0, GROUPS[-1][0], pl.ds(pl.multiple_of(b * COLS, COLS), COLS))
            return carry

        lax.fori_loop(0, 4, step, 0)

    event(0, 1)
    event(1, 1)
    event(2, 1)
    event(3, 1)
    event(0, 2)
    for r in range(NY):
        landed(qbuf.at[r], q_recv.at[r], r)
    near(0, 0, 2)
    event(1, 2)
    event(2, 2)
    near(1, 0, 1)
    event(3, 2)
    near(1, 1, 2)
    event(0, 3)
    near(1, 2, 4)
    near(2, 0, 2)
    event(1, 3)
    near(3, 0, 2)
    event(2, 3)
    event(3, 3)
    event(0, 4)
    event(1, 4)
    far(0, 0, 1)
    event(2, 4)
    far(0, 1, 2)
    event(3, 4)
    far(1, 0, 4)
    far(2, 0, 2)
    far(3, 0, 2)
    copies[4].wait()
    combine(0)
    combine(1)
    combine(2)
    project_early()
    combine(3)

    for copy in copies[5:]:
        copy.wait()

    def branch_part(b, part):
        cols = pl.ds(pl.multiple_of(b * COLS + part * PART, PART), PART)
        return acc[b, :, part * PART : (part + 1) * PART] + project(*GROUPS[-1], cols)

    def sib_copy(i, part):
        return remote(tosib.at[i, part], fromsib.at[i, part], sib_send.at[i, part], sib_recv.at[i, part], sibling)

    def x_copy(part):
        return remote(tox.at[part], fromx.at[part], x_send.at[part], x_recv.at[part], across)

    def stage(i, b):
        for part in range(NP):
            tosib[i, part] = branch_part(b, part).astype(jnp.bfloat16)
            sib_copy(i, part).start()

    stage(0, (1 - xl) * 2 + (1 - core))
    for part in range(NP):
        ours = branch_part((1 - xl) * 2 + core, part)
        sib_copy(0, part).wait_recv()
        tox[part] = (ours + fromsib[0, part].astype(jnp.float32)).astype(jnp.bfloat16)
        x_copy(part).start()
    stage(1, xl * 2 + (1 - core))
    for part in range(NP):
        cols = slice(part * PART, (part + 1) * PART)
        branch = branch_part(tensor, part) + params[0, :, cols]
        sib_copy(1, part).wait_recv()
        mine[part] = hidden[:, cols].astype(jnp.float32) + params[1, :, cols] * (
            branch + fromsib[1, part].astype(jnp.float32)
        )

    total = jnp.zeros((ROWS, HEAD), jnp.float32)
    total_sq = jnp.zeros((ROWS, HEAD), jnp.float32)
    for part in range(NP):
        cols = slice(part * PART, (part + 1) * PART)
        x_copy(part).wait_recv()
        value = mine[part] + params[1, :, cols] * fromx[part].astype(jnp.float32)
        summed[:, cols] = value
        residual[:, cols] = value.astype(jnp.bfloat16)
        for lo in range(0, PART, HEAD):
            piece = value[:, lo : lo + HEAD]
            total = total + piece
            total_sq = total_sq + piece * piece
    stats[0] = columns_to_rows(
        jnp.sum(total, axis=1, keepdims=True), jnp.sum(total_sq, axis=1, keepdims=True)
    )

    def st_copy(r):
        return remote(stats.at[0], stats.at[4 - r], st_send.at[r], st_recv.at[4 - r], tensor_dev(r))

    for r in range(1, 4):
        st_copy(r).start()

    for g in range(NG):
        swap(g, wait=True)
        for up in (True, False):
            for s in range(4):
                hop(g, s, up).wait_send()
        for m in range(len(shares)):
            pair(g, m).wait_send()
        for r in range(NY):
            send_mixed(g, r, wait=True)
    for r in range(NY):
        send_query(r, wait=True)
    for r in range(1, 4):
        sq_copy(r).wait_send()
    for part in range(NP):
        sib_copy(0, part).wait_send()
        sib_copy(1, part).wait_send()
        x_copy(part).wait_send()

    for r in range(1, 4):
        st_copy(4 - r).wait_recv()
    both = jnp.transpose(stats[0] + stats[1] + stats[2] + stats[3]) / D
    mean = both[:, 0:1]
    inv = lax.rsqrt(both[:, 1:2] - mean * mean + 1e-06)
    for part in range(NP):
        cols = slice(part * PART, (part + 1) * PART)
        value = (summed[:, cols] - mean) * inv * (1.0 + params[3, :, cols]) + params[2, :, cols]
        modulated[:, cols] = value.astype(jnp.bfloat16)
    for r in range(1, 4):
        st_copy(r).wait_send()


def deliver(first_in, second_in, first_out, second_out):
    first_out[...] = first_in[...]
    second_out[...] = second_in[...]


def body(
    hidden, query, query_gain, stale_keys, stale_values, out_weight, out_bias, residual_gate, norm_shift, norm_scale
):
    bf16, f32 = jnp.bfloat16, jnp.float32
    vmem = pl.BlockSpec(memory_space=pltpu.VMEM)
    hbm = pl.BlockSpec(memory_space=pltpu.HBM)
    dma = pltpu.SemaphoreType.DMA
    row = lambda x: x.reshape(1, -1)
    out = jax.ShapeDtypeStruct((ROWS, COLS), bf16)
    results = pl.pallas_call(
        kernel,
        out_shape=(out, out),
        in_specs=[hbm] * 10,
        out_specs=(vmem, vmem),
        scratch_shapes=[
            pltpu.VMEM((ROWS, NH * HEAD), bf16),
            pltpu.VMEM((NH * HEAD,), f32),
            pltpu.VMEM((ROWS, NH * HEAD), bf16),
            pltpu.VMEM((ROWS, NH * HEAD), bf16),
            pltpu.VMEM((NH * HEAD, D), bf16),
            pltpu.VMEM((ROWS, COLS), bf16),
            pltpu.VMEM((4, 1, COLS), f32),
            pltpu.VMEM((NH, 2 * ROWS, HEAD), bf16),
            pltpu.VMEM((NH, ROWS, HEAD), bf16),
            pltpu.VMEM((NZ, 2, NH, 2 * ROWS, HEAD), bf16),
            pltpu.VMEM((NY, NH, ROWS, HEAD), bf16),
            pltpu.VMEM((NY, NH, ROWS, HEAD), bf16),
            pltpu.VMEM((NY, NH, ROWS, HEAD), bf16),
            pltpu.VMEM((NY, NH, 8, ROWS), f32),
            pltpu.VMEM((NY, NH, 8, ROWS), f32),
            pltpu.VMEM((NH, 2, 2 * ROWS, HEAD), f32),
            pltpu.VMEM((NH, 2, 2 * ROWS, 1), f32),
            pltpu.VMEM((NH, 2, 2 * ROWS, 1), f32),
            pltpu.VMEM((ROWS, NH * HEAD), bf16),
            pltpu.VMEM((4, ROWS, COLS), f32),
            pltpu.VMEM((4, 8, ROWS), f32),
            pltpu.VMEM((4, 8, ROWS), f32),
            pltpu.VMEM((2, NP, ROWS, PART), bf16),
            pltpu.VMEM((2, NP, ROWS, PART), bf16),
            pltpu.VMEM((NP, ROWS, PART), bf16),
            pltpu.VMEM((NP, ROWS, PART), bf16),
            pltpu.VMEM((NP, ROWS, PART), f32),
            pltpu.VMEM((ROWS, COLS), f32),
            dma((NG,)),
            dma((NG, 2, 4)),
            dma((NG, NZ + 1)),
            dma((NG, 4)),
            dma((NG, 4)),
            dma((NY,)),
            dma((NY,)),
        ]
        + [dma((NG, NY))] * 4
        + [dma((4,))] * 4
        + [dma((2, NP))] * 2
        + [dma((NP,))] * 2
        + [dma((10,))],
        compiler_params=pltpu.CompilerParams(
            collective_id=0, has_side_effects=True, vmem_limit_bytes=56 * 2**20
        ),
        name="attention_block",
    )(
        query, query_gain, stale_keys, stale_values, hidden, out_weight,
        row(out_bias), row(residual_gate), row(norm_shift), row(norm_scale),
    )
    return pl.pallas_call(
        deliver,
        out_shape=(out, out),
        in_specs=[vmem] * 2,
        out_specs=(vmem, vmem),
        compiler_params=pltpu.CompilerParams(vmem_limit_bytes=56 * 2**20),
        name="deliver",
    )(*results)


def solution(mesh):
    return jax.shard_map(
        body,
        mesh=mesh,
        in_specs=(
            P("patch", None),
            P("patch", "tensor"),
            P("tensor"),
            P("patch", "tensor"),
            P("patch", "tensor"),
            P("tensor", None),
            P(),
            P(),
            P(),
            P(),
        ),
        out_specs=(P("patch", "tensor"), P("patch", "tensor")),
        check_vma=False,
    )
```

```python
import functools
import math

import jax
import jax.numpy as jnp
from jax import lax
from jax.experimental import pallas as pl
from jax.experimental.pallas import tpu as pltpu
from jax.sharding import PartitionSpec as P

D = 5120
HEAD = 128
HD = 2560
ROWS = 128
NH = 5
GROUPS = ((0, 1), (1, 2), (3, 1), (4, 1))
NG = len(GROUPS)
NZ = 8
NY = 4
NEAR = 5
COLS = 1280
PART = 256
NP = COLS // PART
MESH = pl.DeviceIdType.MESH
SCALE = HEAD**-0.5 * math.log2(math.e)
CONTRACT_LAST = (((1,), (1,)), ((), ()))


def remote(src, dst, send, recv, device):
    return pltpu.make_async_remote_copy(
        src_ref=src, dst_ref=dst, send_sem=send, recv_sem=recv, device_id=device, device_id_type=MESH
    )


def columns_to_rows(first, second):
    n = first.shape[0]
    lane = lax.broadcasted_iota(jnp.int32, (n, HEAD), 1)
    return jnp.transpose(jnp.where(lane == 0, first, second))[0:8]


def kernel(
    query_hbm, gain_hbm, keys_hbm, values_hbm, hidden_hbm, weight_hbm, bias_hbm, gate_hbm,
    summed_hbm, moments,
    query, gain, keys, values, weight, hidden, params,
    kvstage, qstage, kv, qbuf, osend, orecv, ssend, srecv, near_mix, near_top, near_total, attended, acc,
    sq, stats, tosib, fromsib, tox, fromx, mine, summed,
    swap_send, kv_send, kv_recv, pair_send, pair_recv, q_send, q_recv, o_send, o_recv, s_send, s_recv, sq_send, sq_recv,
    st_send, st_recv, sib_send, sib_recv, x_send, x_recv, local,
):
    patch = lax.axis_index("patch")
    tensor = lax.axis_index("tensor")
    y, z, xh = patch // 16, (patch // 2) % 8, patch % 2
    xl, core = tensor // 2, tensor % 2
    straight = xh == core

    def z_dev(step):
        return {"patch": y * 16 + ((z + step + NZ) % NZ) * 2 + xh, "tensor": tensor}

    def group_dev(r):
        return {"patch": ((y + r) % NY) * 16 + z * 2 + core, "tensor": xl * 2 + xh}

    def tensor_dev(r):
        return {"patch": patch, "tensor": (tensor + r) % 4}

    sibling = {"patch": patch, "tensor": xl * 2 + (1 - core)}
    across = {"patch": patch, "tensor": (1 - xl) * 2 + core}

    barrier = pltpu.get_barrier_semaphore()
    partners = [z_dev(1), z_dev(-1)] + [group_dev(r) for r in range(1, NY)] + [tensor_dev(r) for r in range(1, 4)]
    for device in partners:
        pl.semaphore_signal(barrier, inc=1, device_id=device, device_id_type=MESH)

    @pl.when(jnp.logical_not(straight))
    def _():
        pl.semaphore_signal(barrier, inc=1, device_id=group_dev(0), device_id_type=MESH)

    my_cols = pl.ds(pl.multiple_of(tensor * COLS, COLS), COLS)
    early = [(keys_hbm, keys), (values_hbm, values), (query_hbm, query), (gain_hbm, gain)]
    late = [(weight_hbm, weight), (hidden_hbm.at[:, my_cols], hidden)]
    late += [(ref.at[:, my_cols], params.at[i]) for i, ref in enumerate((bias_hbm, gate_hbm))]
    copies = [pltpu.make_async_copy(src, dst, local.at[i]) for i, (src, dst) in enumerate(early + late)]
    for copy in copies:
        copy.start()

    copies[0].wait()
    copies[1].wait()
    for h in range(NH):
        cols = slice(h * HEAD, (h + 1) * HEAD)
        kvstage[h, 0:ROWS, :] = keys[:, cols]
        kvstage[h, ROWS:, :] = values[:, cols]

    copies[2].wait()
    copies[3].wait()
    q32 = query[...].astype(jnp.float32)
    squares = jnp.sum(q32 * q32, axis=1, keepdims=True)
    sq[0] = columns_to_rows(squares, squares)

    @pl.when(straight)
    def _():
        pl.semaphore_wait(barrier, len(partners))

    @pl.when(jnp.logical_not(straight))
    def _():
        pl.semaphore_wait(barrier, len(partners) + 1)

    def to_group(src, dst, send, recv, r, wait=False):
        copy = remote(src, dst, send, recv, group_dev(r))
        act = copy.wait_send if wait else copy.start
        if r > 0:
            act()
            return
        pl.when(jnp.logical_not(straight))(act)
        if not wait:

            @pl.when(straight)
            def _():
                dst[...] = src[...]

    def landed(ref, recv, r=1):
        wait = remote(ref, ref, swap_send.at[0], recv, z_dev(1)).wait_recv
        if r > 0:
            wait()
        else:
            pl.when(jnp.logical_not(straight))(wait)

    def heads(g):
        return pl.ds(*GROUPS[g])

    def swap(g, wait=False):
        to_group(kvstage.at[heads(g)], kv.at[0, 0, heads(g)], swap_send.at[g], kv_recv.at[g, 0], 0, wait)

    def place(s, up):
        return 0 if s == 0 else 2 * s - 1 if up or s == 4 else 2 * s

    def block(g, s, up):
        if s == 4:
            return kv.at[7, 0, heads(g), pl.ds(0 if up else ROWS, ROWS)]
        return kv.at[place(s, up), 0, heads(g)]

    def block_sem(g, s, up):
        return kv_recv.at[g, 8 if s == 4 and not up else place(s, up)]

    def hop(g, s, up):
        src = block(g, s, up)
        if s == 3:
            src = kv.at[place(s, up), 0, heads(g), pl.ds(0 if up else ROWS, ROWS)]
        return remote(
            src, block(g, s + 1, up), kv_send.at[g, int(up), s], block_sem(g, s + 1, up), z_dev(1 if up else -1)
        )

    shares = ((0, 1), (1, 2), (3, 2), (5, 3))

    def pair(g, m):
        places = pl.ds(*shares[m])
        return remote(
            kv.at[places, 0, heads(g)], kv.at[places, 1, heads(g)], pair_send.at[g, m], pair_recv.at[g, m], sibling
        )

    def event(g, s):
        if s == 0:
            landed(block(g, 0, True), block_sem(g, 0, True), 0)
        for up in (True, False):
            if s > 0:
                landed(block(g, s, up), block_sem(g, s, up))
            if s < 4:
                hop(g, s, up).start()
        if s != 3:
            pair(g, min(s, 3)).start()

    for g in range(min(2, NG)):
        swap(g)

    def sq_copy(r):
        return remote(sq.at[0], sq.at[4 - r], sq_send.at[r], sq_recv.at[4 - r], tensor_dev(r))

    for r in range(1, 4):
        sq_copy(r).start()
    event(0, 0)
    swap(2)
    event(1, 0)
    swap(3)
    for r in range(1, 4):
        sq_copy(4 - r).wait_recv()
    factor = lax.rsqrt((sq[0] + sq[1] + sq[2] + sq[3]) / HD + 1e-06) * SCALE
    factor = jnp.transpose(factor)[:, 0:1]
    normed = (q32 * factor * gain[...][None, :]).astype(jnp.bfloat16)
    for h in range(NH):
        qstage[h] = normed[:, h * HEAD : (h + 1) * HEAD]

    def send_query(r, wait=False):
        back = (NY - r) % NY
        to_group(qstage, qbuf.at[back], q_send.at[r], q_recv.at[back], r, wait)

    for r in range(NY):
        send_query(r)
    event(0, 1)
    event(2, 0)
    event(3, 0)

    def send_mixed(g, r, wait=False):
        back = (NY - r) % NY
        to_group(osend.at[r, heads(g)], orecv.at[back, heads(g)], o_send.at[g, r], o_recv.at[g, back], r, wait)
        to_group(ssend.at[r, heads(g)], srecv.at[back, heads(g)], s_send.at[g, r], s_recv.at[g, back], r, wait)

    def scores_of(h, j, first, count):
        q = qbuf[pl.ds(2 * j, 2), h].reshape(2 * ROWS, HEAD)
        k = kv[first : first + count, :, h, 0:ROWS, :].reshape(count * 2 * ROWS, HEAD)
        return lax.dot_general(q, k, CONTRACT_LAST, preferred_element_type=jnp.float32)

    def mix(h, expo, first, count):
        v = kv[first : first + count, :, h, ROWS : 2 * ROWS, :].reshape(count * 2 * ROWS, HEAD)
        return jnp.dot(expo.astype(jnp.bfloat16), v, preferred_element_type=jnp.float32)

    def lane_sums(x):
        return functools.reduce(jnp.add, [x[:, lo : lo + HEAD] for lo in range(0, x.shape[1], HEAD)])

    def attend_near(h, j):
        scores = scores_of(h, j, 0, NEAR)
        top = jnp.max(scores, axis=1, keepdims=True)
        expo = jnp.exp2(scores - top)
        near_top[h, j] = jnp.broadcast_to(top, (2 * ROWS, HEAD))
        near_total[h, j] = lane_sums(expo)
        near_mix[h, j] = mix(h, expo, 0, NEAR)

    def attend_far(h, j):
        count = NZ - NEAR
        scores = scores_of(h, j, NEAR, count)
        old = near_top[h, j]
        top = jnp.maximum(old, jnp.broadcast_to(jnp.max(scores, axis=1, keepdims=True), (2 * ROWS, HEAD)))
        expo = jnp.exp2(scores - jnp.concatenate([top] * (2 * count), axis=1))
        fade = jnp.exp2(old - top)
        total = jnp.sum(near_total[h, j] * fade + lane_sums(expo), axis=1, keepdims=True)
        mixed = (near_mix[h, j] * fade + mix(h, expo, NEAR, count)).astype(jnp.bfloat16)
        numbers = columns_to_rows(top, total)
        for i in range(2):
            part = slice(i * ROWS, (i + 1) * ROWS)
            osend[2 * j + i, h] = mixed[part]
            ssend[2 * j + i, h] = numbers[:, part]

    def near(g, start, stop):
        if start == 0:
            for m in range(3):
                pair(g, m).wait_recv()
        first, count = GROUPS[g]

        def step(i, carry):
            attend_near(first + i % count, 1 - i // count)
            return carry

        lax.fori_loop(start, stop, step, 0)

    def far(g, start, stop):
        if start == 0:
            pair(g, 3).wait_recv()
        first, count = GROUPS[g]

        def step(i, carry):
            attend_far(first + i % count, 1 - i // count)
            for j in (1, 0):

                @pl.when(i == (2 - j) * count - 1)
                def _(j=j):
                    send_mixed(g, 2 * j + 1)
                    send_mixed(g, 2 * j)

            return carry

        lax.fori_loop(start, stop, step, 0)

    def combine(g):
        for r in range(NY):
            landed(orecv.at[r, heads(g)], o_recv.at[g, r], r)
            landed(srecv.at[r, heads(g)], s_recv.at[g, r], r)
        first, count = GROUPS[g]
        for h in range(first, first + count):
            tops = [srecv[r, h, 0:1, :] for r in range(NY)]
            top = functools.reduce(jnp.maximum, tops)
            shares = [jnp.exp2(t - top) for t in tops]
            den = sum(shares[r] * srecv[r, h, 1:2, :] for r in range(NY))
            scales = jnp.transpose(jnp.concatenate([share / den for share in shares] * 2, axis=0))
            num = sum(scales[:, r : r + 1] * orecv[r, h].astype(jnp.float32) for r in range(NY))
            attended[:, h * HEAD : (h + 1) * HEAD] = num.astype(jnp.bfloat16)

    def project(first, count, columns):
        rows = slice(first * HEAD, (first + count) * HEAD)
        return jnp.dot(attended[:, rows], weight[rows, columns], preferred_element_type=jnp.float32)

    def project_early():
        def step(b, carry):
            acc[b] = project(0, GROUPS[-1][0], pl.ds(pl.multiple_of(b * COLS, COLS), COLS))
            return carry

        lax.fori_loop(0, 4, step, 0)

    event(1, 1)
    event(2, 1)
    event(0, 2)
    event(3, 1)
    for r in range(NY):
        landed(qbuf.at[r], q_recv.at[r], r)
    near(0, 0, 2)
    event(1, 2)
    event(2, 2)
    near(1, 0, 1)
    event(0, 3)
    near(1, 1, 2)
    event(3, 2)
    near(1, 2, 4)
    near(2, 0, 2)
    event(2, 3)
    event(1, 3)
    event(0, 4)
    near(3, 0, 2)
    event(3, 3)
    event(2, 4)
    far(0, 0, 1)
    event(1, 4)
    far(0, 1, 2)
    event(3, 4)
    far(1, 0, 4)
    far(2, 0, 2)
    far(3, 0, 2)
    copies[4].wait()
    combine(0)
    combine(1)
    combine(2)
    project_early()
    combine(3)

    for copy in copies[5:]:
        copy.wait()

    def branch_part(b, part):
        cols = pl.ds(pl.multiple_of(b * COLS + part * PART, PART), PART)
        return acc[b, :, part * PART : (part + 1) * PART] + project(*GROUPS[-1], cols)

    def sib_copy(i, part):
        return remote(tosib.at[i, part], fromsib.at[i, part], sib_send.at[i, part], sib_recv.at[i, part], sibling)

    def x_copy(part):
        return remote(tox.at[part], fromx.at[part], x_send.at[part], x_recv.at[part], across)

    def stage(i, b):
        for part in range(NP):
            tosib[i, part] = branch_part(b, part).astype(jnp.bfloat16)
            sib_copy(i, part).start()

    stage(0, (1 - xl) * 2 + (1 - core))
    for part in range(NP):
        ours = branch_part((1 - xl) * 2 + core, part)
        sib_copy(0, part).wait_recv()
        tox[part] = (ours + fromsib[0, part].astype(jnp.float32)).astype(jnp.bfloat16)
        x_copy(part).start()
    stage(1, xl * 2 + (1 - core))
    for part in range(NP):
        cols = slice(part * PART, (part + 1) * PART)
        branch = branch_part(tensor, part) + params[0, :, cols]
        sib_copy(1, part).wait_recv()
        mine[part] = hidden[:, cols].astype(jnp.float32) + params[1, :, cols] * (
            branch + fromsib[1, part].astype(jnp.float32)
        )

    total = jnp.zeros((ROWS, HEAD), jnp.float32)
    total_sq = jnp.zeros((ROWS, HEAD), jnp.float32)
    for part in range(NP):
        cols = slice(part * PART, (part + 1) * PART)
        x_copy(part).wait_recv()
        value = mine[part] + params[1, :, cols] * fromx[part].astype(jnp.float32)
        summed[:, cols] = value
        for lo in range(0, PART, HEAD):
            piece = value[:, lo : lo + HEAD]
            total = total + piece
            total_sq = total_sq + piece * piece
    keep = pltpu.make_async_copy(summed, summed_hbm, local.at[0])
    keep.start()
    stats[0] = columns_to_rows(
        jnp.sum(total, axis=1, keepdims=True), jnp.sum(total_sq, axis=1, keepdims=True)
    )

    def st_copy(r):
        return remote(stats.at[0], stats.at[4 - r], st_send.at[r], st_recv.at[4 - r], tensor_dev(r))

    for r in range(1, 4):
        st_copy(r).start()

    for g in range(NG):
        swap(g, wait=True)
        for up in (True, False):
            for s in range(4):
                hop(g, s, up).wait_send()
        for m in range(len(shares)):
            pair(g, m).wait_send()
        for r in range(NY):
            send_mixed(g, r, wait=True)
    for r in range(NY):
        send_query(r, wait=True)
    for r in range(1, 4):
        sq_copy(r).wait_send()
    for part in range(NP):
        sib_copy(0, part).wait_send()
        sib_copy(1, part).wait_send()
        x_copy(part).wait_send()

    for r in range(1, 4):
        st_copy(4 - r).wait_recv()
    sums = (stats[0] + stats[1] + stats[2] + stats[3]) / D
    mean = sums[0:1, :]
    moments[...] = jnp.concatenate([mean, lax.rsqrt(sums[1:8, :] - mean * mean + 1e-06)], axis=0)
    keep.wait()
    for r in range(1, 4):
        st_copy(r).wait_send()


def normalise(summed, moments, shift, scale, residual, modulated):
    columns = jnp.transpose(moments[...])
    mean, inv = columns[:, 0:1], columns[:, 1:2]
    my_cols = pl.ds(pl.multiple_of(lax.axis_index("tensor") * COLS, COLS), COLS)
    value = summed[...]
    residual[...] = value.astype(jnp.bfloat16)
    modulated[...] = ((value - mean) * inv * (1.0 + scale[:, my_cols]) + shift[:, my_cols]).astype(jnp.bfloat16)


def body(
    hidden, query, query_gain, stale_keys, stale_values, out_weight, out_bias, residual_gate, norm_shift, norm_scale
):
    bf16, f32 = jnp.bfloat16, jnp.float32
    vmem = pl.BlockSpec(memory_space=pltpu.VMEM)
    hbm = pl.BlockSpec(memory_space=pltpu.HBM)
    dma = pltpu.SemaphoreType.DMA
    row = lambda x: x.reshape(1, -1)
    out = jax.ShapeDtypeStruct((ROWS, COLS), bf16)
    summed, moments = pl.pallas_call(
        kernel,
        out_shape=(jax.ShapeDtypeStruct((ROWS, COLS), f32), jax.ShapeDtypeStruct((8, ROWS), f32)),
        in_specs=[hbm] * 8,
        out_specs=(hbm, vmem),
        scratch_shapes=[
            pltpu.VMEM((ROWS, NH * HEAD), bf16),
            pltpu.VMEM((NH * HEAD,), f32),
            pltpu.VMEM((ROWS, NH * HEAD), bf16),
            pltpu.VMEM((ROWS, NH * HEAD), bf16),
            pltpu.VMEM((NH * HEAD, D), bf16),
            pltpu.VMEM((ROWS, COLS), bf16),
            pltpu.VMEM((2, 1, COLS), f32),
            pltpu.VMEM((NH, 2 * ROWS, HEAD), bf16),
            pltpu.VMEM((NH, ROWS, HEAD), bf16),
            pltpu.VMEM((NZ, 2, NH, 2 * ROWS, HEAD), bf16),
            pltpu.VMEM((NY, NH, ROWS, HEAD), bf16),
            pltpu.VMEM((NY, NH, ROWS, HEAD), bf16),
            pltpu.VMEM((NY, NH, ROWS, HEAD), bf16),
            pltpu.VMEM((NY, NH, 8, ROWS), f32),
            pltpu.VMEM((NY, NH, 8, ROWS), f32),
            pltpu.VMEM((NH, 2, 2 * ROWS, HEAD), f32),
            pltpu.VMEM((NH, 2, 2 * ROWS, HEAD), f32),
            pltpu.VMEM((NH, 2, 2 * ROWS, HEAD), f32),
            pltpu.VMEM((ROWS, NH * HEAD), bf16),
            pltpu.VMEM((4, ROWS, COLS), f32),
            pltpu.VMEM((4, 8, ROWS), f32),
            pltpu.VMEM((4, 8, ROWS), f32),
            pltpu.VMEM((2, NP, ROWS, PART), bf16),
            pltpu.VMEM((2, NP, ROWS, PART), bf16),
            pltpu.VMEM((NP, ROWS, PART), bf16),
            pltpu.VMEM((NP, ROWS, PART), bf16),
            pltpu.VMEM((NP, ROWS, PART), f32),
            pltpu.VMEM((ROWS, COLS), f32),
            dma((NG,)),
            dma((NG, 2, 4)),
            dma((NG, NZ + 1)),
            dma((NG, 4)),
            dma((NG, 4)),
            dma((NY,)),
            dma((NY,)),
        ]
        + [dma((NG, NY))] * 4
        + [dma((4,))] * 4
        + [dma((2, NP))] * 2
        + [dma((NP,))] * 2
        + [dma((8,))],
        compiler_params=pltpu.CompilerParams(
            collective_id=0, has_side_effects=True, vmem_limit_bytes=56 * 2**20
        ),
        name="attention_block",
    )(
        query, query_gain, stale_keys, stale_values, hidden, out_weight,
        row(out_bias), row(residual_gate),
    )
    return pl.pallas_call(
        normalise,
        out_shape=(out, out),
        in_specs=[vmem] * 4,
        out_specs=(vmem, vmem),
        compiler_params=pltpu.CompilerParams(vmem_limit_bytes=56 * 2**20),
        name="normalise",
    )(summed, moments, row(norm_shift), row(norm_scale))


def solution(mesh):
    return jax.shard_map(
        body,
        mesh=mesh,
        in_specs=(
            P("patch", None),
            P("patch", "tensor"),
            P("tensor"),
            P("patch", "tensor"),
            P("patch", "tensor"),
            P("tensor", None),
            P(),
            P(),
            P(),
            P(),
        ),
        out_specs=(P("patch", "tensor"), P("patch", "tensor")),
        check_vma=False,
    )
```

```python
import functools
import math

import jax
import jax.numpy as jnp
from jax import lax
from jax.experimental import pallas as pl
from jax.experimental.pallas import tpu as pltpu
from jax.sharding import PartitionSpec as P

D = 5120
HEAD = 128
HD = 2560
ROWS = 128
NH = 5
GROUPS = ((0, 1), (1, 2), (3, 1), (4, 1))
NG = len(GROUPS)
NZ = 8
NY = 4
NEAR = 5
HALF = ROWS // 2
BOTH = 2
COLS = 1280
PART = 256
NP = COLS // PART
MESH = pl.DeviceIdType.MESH
SCALE = HEAD**-0.5 * math.log2(math.e)
CONTRACT_LAST = (((1,), (1,)), ((), ()))


def remote(src, dst, send, recv, device):
    return pltpu.make_async_remote_copy(
        src_ref=src, dst_ref=dst, send_sem=send, recv_sem=recv, device_id=device, device_id_type=MESH
    )


def columns_to_rows(first, second):
    n = first.shape[0]
    lane = lax.broadcasted_iota(jnp.int32, (n, HEAD), 1)
    return jnp.transpose(jnp.where(lane == 0, first, second))[0:8]


def kernel(
    query_hbm, gain_hbm, keys_hbm, values_hbm, hidden_hbm, weight_hbm, bias_hbm, gate_hbm,
    summed_hbm, moments,
    query, gain, keys, values, weight, hidden, params,
    kvstage, qstage, kv, qbuf, osend, orecv, ssend, srecv, near_mix, near_top, near_total, attended, crossing, otwin, stwin, acc,
    sq, stats, tosib, fromsib, tox, fromx, mine, summed,
    swap_send, kv_send, kv_recv, pair_send, pair_recv, q_send, q_recv, o_send, o_recv, s_send, s_recv, sq_send, sq_recv,
    st_send, st_recv, sib_send, sib_recv, x_send, x_recv, ot_send, ot_recv, stt_send, stt_recv, half_send, half_recv, local,
):
    patch = lax.axis_index("patch")
    tensor = lax.axis_index("tensor")
    y, z, xh = patch // 16, (patch // 2) % 8, patch % 2
    xl, core = tensor // 2, tensor % 2
    straight = xh == core

    def z_dev(step):
        return {"patch": y * 16 + ((z + step + NZ) % NZ) * 2 + xh, "tensor": tensor}

    def group_dev(r):
        return {"patch": ((y + r) % NY) * 16 + z * 2 + core, "tensor": xl * 2 + xh}

    def tensor_dev(r):
        return {"patch": patch, "tensor": (tensor + r) % 4}

    sibling = {"patch": patch, "tensor": xl * 2 + (1 - core)}
    across = {"patch": patch, "tensor": (1 - xl) * 2 + core}

    def twin_like(r):
        return {"patch": ((y + r) % NY) * 16 + z * 2 + (1 - xh), "tensor": tensor}

    def sibling_like(r):
        return {"patch": ((y + r) % NY) * 16 + z * 2 + xh, "tensor": xl * 2 + (1 - core)}

    def group_twin(r):
        return {"patch": ((y + r) % NY) * 16 + z * 2 + (1 - core), "tensor": xl * 2 + xh}

    twin = twin_like(0)
    across_twin = {"patch": y * 16 + z * 2 + (1 - xh), "tensor": (1 - xl) * 2 + core}

    barrier = pltpu.get_barrier_semaphore()
    partners = [z_dev(1), z_dev(-1)] + [group_dev(r) for r in range(1, NY)] + [tensor_dev(r) for r in range(1, 4)]
    partners += [twin_like(r) for r in range(NY)] + [sibling_like(r) for r in range(1, NY)] + [across_twin]
    for device in partners:
        pl.semaphore_signal(barrier, inc=1, device_id=device, device_id_type=MESH)

    @pl.when(jnp.logical_not(straight))
    def _():
        pl.semaphore_signal(barrier, inc=1, device_id=group_dev(0), device_id_type=MESH)

    my_cols = pl.ds(pl.multiple_of(tensor * COLS, COLS), COLS)
    early = [(keys_hbm, keys), (values_hbm, values), (query_hbm, query), (gain_hbm, gain)]
    late = [(weight_hbm, weight), (hidden_hbm.at[:, my_cols], hidden)]
    late += [(ref.at[:, my_cols], params.at[i]) for i, ref in enumerate((bias_hbm, gate_hbm))]
    copies = [pltpu.make_async_copy(src, dst, local.at[i]) for i, (src, dst) in enumerate(early + late)]
    for copy in copies:
        copy.start()

    copies[0].wait()
    copies[1].wait()
    for h in range(NH):
        cols = slice(h * HEAD, (h + 1) * HEAD)
        kvstage[h, 0:ROWS, :] = keys[:, cols]
        kvstage[h, ROWS:, :] = values[:, cols]

    copies[2].wait()
    copies[3].wait()
    q32 = query[...].astype(jnp.float32)
    squares = jnp.sum(q32 * q32, axis=1, keepdims=True)
    sq[0] = columns_to_rows(squares, squares)

    @pl.when(straight)
    def _():
        pl.semaphore_wait(barrier, len(partners))

    @pl.when(jnp.logical_not(straight))
    def _():
        pl.semaphore_wait(barrier, len(partners) + 1)

    def to_group(src, dst, send, recv, r, wait=False):
        copy = remote(src, dst, send, recv, group_dev(r))
        act = copy.wait_send if wait else copy.start
        if r > 0:
            act()
            return
        pl.when(jnp.logical_not(straight))(act)
        if not wait:

            @pl.when(straight)
            def _():
                dst[...] = src[...]

    def landed(ref, recv, r=1):
        wait = remote(ref, ref, swap_send.at[0], recv, z_dev(1)).wait_recv
        if r > 0:
            wait()
        else:
            pl.when(jnp.logical_not(straight))(wait)

    def heads(g):
        return pl.ds(*GROUPS[g])

    def swap(g, wait=False):
        to_group(kvstage.at[heads(g)], kv.at[0, 0, heads(g)], swap_send.at[g], kv_recv.at[g, 0], 0, wait)

    def place(s, up):
        return 0 if s == 0 else 2 * s - 1 if up or s == 4 else 2 * s

    def block(g, s, up):
        if s == 4:
            return kv.at[7, 0, heads(g), pl.ds(0 if up else ROWS, ROWS)]
        return kv.at[place(s, up), 0, heads(g)]

    def block_sem(g, s, up):
        return kv_recv.at[g, 8 if s == 4 and not up else place(s, up)]

    def hop(g, s, up):
        src = block(g, s, up)
        if s == 3:
            src = kv.at[place(s, up), 0, heads(g), pl.ds(0 if up else ROWS, ROWS)]
        return remote(
            src, block(g, s + 1, up), kv_send.at[g, int(up), s], block_sem(g, s + 1, up), z_dev(1 if up else -1)
        )

    shares = ((0, 1), (1, 2), (3, 2), (5, 3))

    def pair(g, m):
        places = pl.ds(*shares[m])
        return remote(
            kv.at[places, 0, heads(g)], kv.at[places, 1, heads(g)], pair_send.at[g, m], pair_recv.at[g, m], sibling
        )

    def event(g, s):
        if s == 0:
            landed(block(g, 0, True), block_sem(g, 0, True), 0)
        for up in (True, False):
            if s > 0:
                landed(block(g, s, up), block_sem(g, s, up))
            if s < 4:
                hop(g, s, up).start()
        if s != 3:
            pair(g, min(s, 3)).start()

    for g in range(min(2, NG)):
        swap(g)

    def sq_copy(r):
        return remote(sq.at[0], sq.at[4 - r], sq_send.at[r], sq_recv.at[4 - r], tensor_dev(r))

    for r in range(1, 4):
        sq_copy(r).start()
    event(0, 0)
    swap(2)
    event(1, 0)
    swap(3)
    for r in range(1, 4):
        sq_copy(4 - r).wait_recv()
    factor = lax.rsqrt((sq[0] + sq[1] + sq[2] + sq[3]) / HD + 1e-06) * SCALE
    factor = jnp.transpose(factor)[:, 0:1]
    normed = (q32 * factor * gain[...][None, :]).astype(jnp.bfloat16)
    for h in range(NH):
        qstage[h] = normed[:, h * HEAD : (h + 1) * HEAD]

    def send_query(r, wait=False):
        back = (NY - r) % NY
        to_group(qstage, qbuf.at[back], q_send.at[r], q_recv.at[back], r, wait)

    for r in range(NY):
        send_query(r)
    event(0, 1)
    event(2, 0)
    event(3, 0)

    def send_mixed(g, r, wait=False):
        back = (NY - r) % NY
        to_group(osend.at[r, heads(g)], orecv.at[back, heads(g)], o_send.at[g, r], o_recv.at[g, back], r, wait)
        to_group(ssend.at[r, heads(g)], srecv.at[back, heads(g)], s_send.at[g, r], s_recv.at[g, back], r, wait)

    def to_twin(g, r):
        (h, _), i, back = GROUPS[g], g - BOTH, (NY - r) % NY
        return (
            remote(osend.at[r, h, pl.ds(HALF, HALF)], otwin.at[i, back], ot_send.at[i, r], ot_recv.at[i, back], group_twin(r)),
            remote(ssend.at[r, h], stwin.at[i, back], stt_send.at[i, r], stt_recv.at[i, back], group_twin(r)),
        )

    def scores_of(h, j, first, count):
        q = qbuf[pl.ds(2 * j, 2), h].reshape(2 * ROWS, HEAD)
        k = kv[first : first + count, :, h, 0:ROWS, :].reshape(count * 2 * ROWS, HEAD)
        return lax.dot_general(q, k, CONTRACT_LAST, preferred_element_type=jnp.float32)

    def mix(h, expo, first, count):
        v = kv[first : first + count, :, h, ROWS : 2 * ROWS, :].reshape(count * 2 * ROWS, HEAD)
        return jnp.dot(expo.astype(jnp.bfloat16), v, preferred_element_type=jnp.float32)

    def lane_sums(x):
        return functools.reduce(jnp.add, [x[:, lo : lo + HEAD] for lo in range(0, x.shape[1], HEAD)])

    def attend_near(h, j):
        scores = scores_of(h, j, 0, NEAR)
        top = jnp.max(scores, axis=1, keepdims=True)
        expo = jnp.exp2(scores - top)
        near_top[h, j] = jnp.broadcast_to(top, (2 * ROWS, HEAD))
        near_total[h, j] = lane_sums(expo)
        near_mix[h, j] = mix(h, expo, 0, NEAR)

    def attend_far(h, j):
        count = NZ - NEAR
        scores = scores_of(h, j, NEAR, count)
        old = near_top[h, j]
        top = jnp.maximum(old, jnp.broadcast_to(jnp.max(scores, axis=1, keepdims=True), (2 * ROWS, HEAD)))
        expo = jnp.exp2(scores - jnp.concatenate([top] * (2 * count), axis=1))
        fade = jnp.exp2(old - top)
        total = jnp.sum(near_total[h, j] * fade + lane_sums(expo), axis=1, keepdims=True)
        mixed = (near_mix[h, j] * fade + mix(h, expo, NEAR, count)).astype(jnp.bfloat16)
        numbers = columns_to_rows(top, total)
        for i in range(2):
            part = slice(i * ROWS, (i + 1) * ROWS)
            osend[2 * j + i, h] = mixed[part]
            ssend[2 * j + i, h] = numbers[:, part]

    def near(g, start, stop):
        if start == 0:
            for m in range(3):
                pair(g, m).wait_recv()
        first, count = GROUPS[g]

        def step(i, carry):
            attend_near(first + i % count, 1 - i // count)
            return carry

        lax.fori_loop(start, stop, step, 0)

    def far(g, start, stop):
        if start == 0:
            pair(g, 3).wait_recv()
        first, count = GROUPS[g]

        def step(i, carry):
            attend_far(first + i % count, 1 - i // count)
            for j in (1, 0):

                @pl.when(i == (2 - j) * count - 1)
                def _(j=j):
                    for r in (2 * j + 1, 2 * j):
                        send_mixed(g, r)
                        if g >= BOTH:
                            for copy in to_twin(g, r):
                                copy.start()

            return carry

        lax.fori_loop(start, stop, step, 0)

    def merge_scales(numbers):
        tops = [x[0:1, :] for x in numbers]
        top = functools.reduce(jnp.maximum, tops)
        shares = [jnp.exp2(t - top) for t in tops]
        den = sum(share * x[1:2, :] for share, x in zip(shares, numbers))
        return jnp.transpose(jnp.concatenate([share / den for share in shares] * 2, axis=0))

    def combine(g):
        for r in range(NY):
            landed(orecv.at[r, heads(g)], o_recv.at[g, r], r)
            landed(srecv.at[r, heads(g)], s_recv.at[g, r], r)
        first, count = GROUPS[g]
        for h in range(first, first + count):
            scales = merge_scales([srecv[r, h] for r in range(NY)])
            num = sum(scales[:, r : r + 1] * orecv[r, h].astype(jnp.float32) for r in range(NY))
            attended[:, h * HEAD : (h + 1) * HEAD] = num.astype(jnp.bfloat16)

    def combine_twin(g):
        (h, _), i = GROUPS[g], g - BOTH
        for r in range(NY):
            landed(otwin.at[i, r], ot_recv.at[i, r])
            landed(stwin.at[i, r], stt_recv.at[i, r])
        scales = merge_scales([stwin[i, r] for r in range(NY)])[HALF:]
        num = sum(scales[:, r : r + 1] * otwin[i, r].astype(jnp.float32) for r in range(NY))
        crossing[HALF:, h * HEAD : (h + 1) * HEAD] = num.astype(jnp.bfloat16)
        crossing[0:HALF, h * HEAD : (h + 1) * HEAD] = attended[0:HALF, h * HEAD : (h + 1) * HEAD]

    first_lanes = pl.ds(0, GROUPS[BOTH][0] * HEAD)

    def half_copy():
        return remote(
            attended.at[pl.ds(HALF, HALF), first_lanes], crossing.at[pl.ds(HALF, HALF), first_lanes],
            half_send.at[0], half_recv.at[0], twin,
        )

    def project(source, first, count, columns):
        rows = slice(first * HEAD, (first + count) * HEAD)
        return jnp.dot(source[:, rows], weight[rows, columns], preferred_element_type=jnp.float32)

    def project_early(source, chip):
        def step(i, carry):
            b = chip * 2 + i
            acc[b] = project(source, 0, NH - 1, pl.ds(pl.multiple_of(b * COLS, COLS), COLS))
            return carry

        lax.fori_loop(0, 2, step, 0)

    event(1, 1)
    event(2, 1)
    event(0, 2)
    event(3, 1)
    for r in range(NY):
        landed(qbuf.at[r], q_recv.at[r], r)
    near(0, 0, 2)
    event(1, 2)
    event(2, 2)
    near(1, 0, 1)
    event(0, 3)
    near(1, 1, 2)
    event(3, 2)
    near(1, 2, 4)
    near(2, 0, 2)
    event(2, 3)
    event(1, 3)
    event(0, 4)
    near(3, 0, 2)
    event(3, 3)
    event(2, 4)
    far(0, 0, 1)
    event(1, 4)
    far(0, 1, 2)
    event(3, 4)
    far(1, 0, 4)
    far(2, 0, 2)
    far(3, 0, 2)
    copies[4].wait()
    combine(0)
    combine(1)
    half_copy().start()
    crossing[0:HALF, 0 : GROUPS[BOTH][0] * HEAD] = attended[0:HALF, 0 : GROUPS[BOTH][0] * HEAD]
    combine(2)
    combine_twin(2)
    project_early(attended, xl)
    half_copy().wait_recv()
    project_early(crossing, 1 - xl)
    combine(3)
    combine_twin(3)

    for copy in copies[5:]:
        copy.wait()

    def branch_part(source, b, part):
        cols = pl.ds(pl.multiple_of(b * COLS + part * PART, PART), PART)
        return acc[b, :, part * PART : (part + 1) * PART] + project(source, NH - 1, 1, cols)

    def sib_copy(i, part):
        return remote(tosib.at[i, part], fromsib.at[i, part], sib_send.at[i, part], sib_recv.at[i, part], sibling)

    def x_copies(part):
        halves = pl.ds(0, HALF), pl.ds(HALF, HALF)
        return [
            remote(tox.at[part, half], fromx.at[part, half], x_send.at[i, part], x_recv.at[i, part], device)
            for i, (half, device) in enumerate(zip(halves, (across, across_twin)))
        ]

    def stage(i, source, b):
        for part in range(NP):
            tosib[i, part] = branch_part(source, b, part).astype(jnp.bfloat16)
            sib_copy(i, part).start()

    stage(0, crossing, (1 - xl) * 2 + (1 - core))
    for part in range(NP):
        ours = branch_part(crossing, (1 - xl) * 2 + core, part)
        sib_copy(0, part).wait_recv()
        tox[part] = (ours + fromsib[0, part].astype(jnp.float32)).astype(jnp.bfloat16)
        for copy in x_copies(part):
            copy.start()
    stage(1, attended, xl * 2 + (1 - core))
    for part in range(NP):
        cols = slice(part * PART, (part + 1) * PART)
        branch = branch_part(attended, tensor, part) + params[0, :, cols]
        sib_copy(1, part).wait_recv()
        mine[part] = hidden[:, cols].astype(jnp.float32) + params[1, :, cols] * (
            branch + fromsib[1, part].astype(jnp.float32)
        )

    total = jnp.zeros((ROWS, HEAD), jnp.float32)
    total_sq = jnp.zeros((ROWS, HEAD), jnp.float32)
    for part in range(NP):
        cols = slice(part * PART, (part + 1) * PART)
        for copy in x_copies(part):
            copy.wait_recv()
        value = mine[part] + params[1, :, cols] * fromx[part].astype(jnp.float32)
        summed[:, cols] = value
        for lo in range(0, PART, HEAD):
            piece = value[:, lo : lo + HEAD]
            total = total + piece
            total_sq = total_sq + piece * piece
    keep = pltpu.make_async_copy(summed, summed_hbm, local.at[0])
    keep.start()
    stats[0] = columns_to_rows(
        jnp.sum(total, axis=1, keepdims=True), jnp.sum(total_sq, axis=1, keepdims=True)
    )

    def st_copy(r):
        return remote(stats.at[0], stats.at[4 - r], st_send.at[r], st_recv.at[4 - r], tensor_dev(r))

    for r in range(1, 4):
        st_copy(r).start()

    for g in range(NG):
        swap(g, wait=True)
        for up in (True, False):
            for s in range(4):
                hop(g, s, up).wait_send()
        for m in range(len(shares)):
            pair(g, m).wait_send()
        for r in range(NY):
            send_mixed(g, r, wait=True)
            if g >= BOTH:
                for copy in to_twin(g, r):
                    copy.wait_send()
    for r in range(NY):
        send_query(r, wait=True)
    half_copy().wait_send()
    for r in range(1, 4):
        sq_copy(r).wait_send()
    for part in range(NP):
        sib_copy(0, part).wait_send()
        sib_copy(1, part).wait_send()
        for copy in x_copies(part):
            copy.wait_send()

    for r in range(1, 4):
        st_copy(4 - r).wait_recv()
    sums = (stats[0] + stats[1] + stats[2] + stats[3]) / D
    mean = sums[0:1, :]
    moments[...] = jnp.concatenate([mean, lax.rsqrt(sums[1:8, :] - mean * mean + 1e-06)], axis=0)
    keep.wait()
    for r in range(1, 4):
        st_copy(r).wait_send()


def normalise(summed, moments, shift, scale, residual, modulated):
    columns = jnp.transpose(moments[...])
    mean, inv = columns[:, 0:1], columns[:, 1:2]
    my_cols = pl.ds(pl.multiple_of(lax.axis_index("tensor") * COLS, COLS), COLS)
    value = summed[...]
    residual[...] = value.astype(jnp.bfloat16)
    modulated[...] = ((value - mean) * inv * (1.0 + scale[:, my_cols]) + shift[:, my_cols]).astype(jnp.bfloat16)


def body(
    hidden, query, query_gain, stale_keys, stale_values, out_weight, out_bias, residual_gate, norm_shift, norm_scale
):
    bf16, f32 = jnp.bfloat16, jnp.float32
    vmem = pl.BlockSpec(memory_space=pltpu.VMEM)
    hbm = pl.BlockSpec(memory_space=pltpu.HBM)
    dma = pltpu.SemaphoreType.DMA
    row = lambda x: x.reshape(1, -1)
    out = jax.ShapeDtypeStruct((ROWS, COLS), bf16)
    summed, moments = pl.pallas_call(
        kernel,
        out_shape=(jax.ShapeDtypeStruct((ROWS, COLS), f32), jax.ShapeDtypeStruct((8, ROWS), f32)),
        in_specs=[hbm] * 8,
        out_specs=(hbm, vmem),
        scratch_shapes=[
            pltpu.VMEM((ROWS, NH * HEAD), bf16),
            pltpu.VMEM((NH * HEAD,), f32),
            pltpu.VMEM((ROWS, NH * HEAD), bf16),
            pltpu.VMEM((ROWS, NH * HEAD), bf16),
            pltpu.VMEM((NH * HEAD, D), bf16),
            pltpu.VMEM((ROWS, COLS), bf16),
            pltpu.VMEM((2, 1, COLS), f32),
            pltpu.VMEM((NH, 2 * ROWS, HEAD), bf16),
            pltpu.VMEM((NH, ROWS, HEAD), bf16),
            pltpu.VMEM((NZ, 2, NH, 2 * ROWS, HEAD), bf16),
            pltpu.VMEM((NY, NH, ROWS, HEAD), bf16),
            pltpu.VMEM((NY, NH, ROWS, HEAD), bf16),
            pltpu.VMEM((NY, NH, ROWS, HEAD), bf16),
            pltpu.VMEM((NY, NH, 8, ROWS), f32),
            pltpu.VMEM((NY, NH, 8, ROWS), f32),
            pltpu.VMEM((NH, 2, 2 * ROWS, HEAD), f32),
            pltpu.VMEM((NH, 2, 2 * ROWS, HEAD), f32),
            pltpu.VMEM((NH, 2, 2 * ROWS, HEAD), f32),
            pltpu.VMEM((ROWS, NH * HEAD), bf16),
            pltpu.VMEM((ROWS, NH * HEAD), bf16),
            pltpu.VMEM((NG - BOTH, NY, HALF, HEAD), bf16),
            pltpu.VMEM((NG - BOTH, NY, 8, ROWS), f32),
            pltpu.VMEM((4, ROWS, COLS), f32),
            pltpu.VMEM((4, 8, ROWS), f32),
            pltpu.VMEM((4, 8, ROWS), f32),
            pltpu.VMEM((2, NP, ROWS, PART), bf16),
            pltpu.VMEM((2, NP, ROWS, PART), bf16),
            pltpu.VMEM((NP, ROWS, PART), bf16),
            pltpu.VMEM((NP, ROWS, PART), bf16),
            pltpu.VMEM((NP, ROWS, PART), f32),
            pltpu.VMEM((ROWS, COLS), f32),
            dma((NG,)),
            dma((NG, 2, 4)),
            dma((NG, NZ + 1)),
            dma((NG, 4)),
            dma((NG, 4)),
            dma((NY,)),
            dma((NY,)),
        ]
        + [dma((NG, NY))] * 4
        + [dma((4,))] * 4
        + [dma((2, NP))] * 2
        + [dma((2, NP))] * 2
        + [dma((NG - BOTH, NY))] * 4
        + [dma((1,))] * 2
        + [dma((8,))],
        compiler_params=pltpu.CompilerParams(
            collective_id=0, has_side_effects=True, vmem_limit_bytes=56 * 2**20
        ),
        name="attention_block",
    )(
        query, query_gain, stale_keys, stale_values, hidden, out_weight,
        row(out_bias), row(residual_gate),
    )
    return pl.pallas_call(
        normalise,
        out_shape=(out, out),
        in_specs=[vmem] * 4,
        out_specs=(vmem, vmem),
        compiler_params=pltpu.CompilerParams(vmem_limit_bytes=56 * 2**20),
        name="normalise",
    )(summed, moments, row(norm_shift), row(norm_scale))


def solution(mesh):
    return jax.shard_map(
        body,
        mesh=mesh,
        in_specs=(
            P("patch", None),
            P("patch", "tensor"),
            P("tensor"),
            P("patch", "tensor"),
            P("patch", "tensor"),
            P("tensor", None),
            P(),
            P(),
            P(),
            P(),
        ),
        out_specs=(P("patch", "tensor"), P("patch", "tensor")),
        check_vma=False,
    )
```

```python
import functools
import math

import jax
import jax.numpy as jnp
from jax import lax
from jax.experimental import pallas as pl
from jax.experimental.pallas import tpu as pltpu
from jax.sharding import PartitionSpec as P

D = 5120
HEAD = 128
HD = 2560
ROWS = 128
NH = 5
GROUPS = ((0, 1), (1, 1), (2, 2), (4, 1))
NG = len(GROUPS)
NZ = 8
NY = 4
PARTS = ((0, 3), (3, 2), (5, 2), (7, 1))
COLS = 1280
PART = 256
NP = COLS // PART
MESH = pl.DeviceIdType.MESH
SCALE = HEAD**-0.5 * math.log2(math.e)
CONTRACT_LAST = (((1,), (1,)), ((), ()))


def remote(src, dst, send, recv, device):
    return pltpu.make_async_remote_copy(
        src_ref=src, dst_ref=dst, send_sem=send, recv_sem=recv, device_id=device, device_id_type=MESH
    )


def columns_to_rows(first, second):
    n = first.shape[0]
    lane = lax.broadcasted_iota(jnp.int32, (n, HEAD), 1)
    return jnp.transpose(jnp.where(lane == 0, first, second))[0:8]


def kernel(
    query_hbm, gain_hbm, keys_hbm, values_hbm, hidden_hbm, weight_hbm, bias_hbm, gate_hbm,
    summed_hbm, moments,
    query, gain, keys, values, weight, hidden, params,
    kvstage, qstage, kv, qbuf, osend, orecv, ssend, srecv, run_mix, run_top, run_total, attended, acc,
    sq, stats, tosib, fromsib, tox, fromx, mine, summed,
    swap_send, kv_send, kv_recv, pair_send, pair_recv, q_send, q_recv, o_send, o_recv, s_send, s_recv, sq_send, sq_recv,
    st_send, st_recv, sib_send, sib_recv, x_send, x_recv, local,
):
    patch = lax.axis_index("patch")
    tensor = lax.axis_index("tensor")
    y, z, xh = patch // 16, (patch // 2) % 8, patch % 2
    xl, core = tensor // 2, tensor % 2
    straight = xh == core

    def z_dev(step):
        return {"patch": y * 16 + ((z + step + NZ) % NZ) * 2 + xh, "tensor": tensor}

    def group_dev(r):
        return {"patch": ((y + r) % NY) * 16 + z * 2 + core, "tensor": xl * 2 + xh}

    def tensor_dev(r):
        return {"patch": patch, "tensor": (tensor + r) % 4}

    sibling = {"patch": patch, "tensor": xl * 2 + (1 - core)}
    across = {"patch": patch, "tensor": (1 - xl) * 2 + core}

    barrier = pltpu.get_barrier_semaphore()
    partners = [z_dev(1), z_dev(-1)] + [group_dev(r) for r in range(1, NY)] + [tensor_dev(r) for r in range(1, 4)]
    for device in partners:
        pl.semaphore_signal(barrier, inc=1, device_id=device, device_id_type=MESH)

    @pl.when(jnp.logical_not(straight))
    def _():
        pl.semaphore_signal(barrier, inc=1, device_id=group_dev(0), device_id_type=MESH)

    my_cols = pl.ds(pl.multiple_of(tensor * COLS, COLS), COLS)
    early = [(keys_hbm, keys), (values_hbm, values), (query_hbm, query), (gain_hbm, gain)]
    late = [(weight_hbm, weight), (hidden_hbm.at[:, my_cols], hidden)]
    late += [(ref.at[:, my_cols], params.at[i]) for i, ref in enumerate((bias_hbm, gate_hbm))]
    copies = [pltpu.make_async_copy(src, dst, local.at[i]) for i, (src, dst) in enumerate(early + late)]
    for copy in copies:
        copy.start()

    copies[0].wait()
    copies[1].wait()
    for h in range(NH):
        cols = slice(h * HEAD, (h + 1) * HEAD)
        kvstage[h, 0:ROWS, :] = keys[:, cols]
        kvstage[h, ROWS:, :] = values[:, cols]

    copies[2].wait()
    copies[3].wait()
    q32 = query[...].astype(jnp.float32)
    squares = jnp.sum(q32 * q32, axis=1, keepdims=True)
    sq[0] = columns_to_rows(squares, squares)

    @pl.when(straight)
    def _():
        pl.semaphore_wait(barrier, len(partners))

    @pl.when(jnp.logical_not(straight))
    def _():
        pl.semaphore_wait(barrier, len(partners) + 1)

    def to_group(src, dst, send, recv, r, wait=False):
        copy = remote(src, dst, send, recv, group_dev(r))
        act = copy.wait_send if wait else copy.start
        if r > 0:
            act()
            return
        pl.when(jnp.logical_not(straight))(act)
        if not wait:

            @pl.when(straight)
            def _():
                dst[...] = src[...]

    def landed(ref, recv, r=1):
        wait = remote(ref, ref, swap_send.at[0], recv, z_dev(1)).wait_recv
        if r > 0:
            wait()
        else:
            pl.when(jnp.logical_not(straight))(wait)

    def heads(g):
        return pl.ds(*GROUPS[g])

    def swap(g, wait=False):
        to_group(kvstage.at[heads(g)], kv.at[0, 0, heads(g)], swap_send.at[g], kv_recv.at[g, 0], 0, wait)

    def place(s, up):
        return 0 if s == 0 else 2 * s - 1 if up or s == 4 else 2 * s

    def block(g, s, up):
        if s == 4:
            return kv.at[7, 0, heads(g), pl.ds(0 if up else ROWS, ROWS)]
        return kv.at[place(s, up), 0, heads(g)]

    def block_sem(g, s, up):
        return kv_recv.at[g, 8 if s == 4 and not up else place(s, up)]

    def hop(g, s, up):
        src = block(g, s, up)
        if s == 3:
            src = kv.at[place(s, up), 0, heads(g), pl.ds(0 if up else ROWS, ROWS)]
        return remote(
            src, block(g, s + 1, up), kv_send.at[g, int(up), s], block_sem(g, s + 1, up), z_dev(1 if up else -1)
        )

    shares = ((0, 1), (1, 2), (3, 2), (5, 2), (7, 1))

    def pair(g, m):
        places = pl.ds(*shares[m])
        return remote(
            kv.at[places, 0, heads(g)], kv.at[places, 1, heads(g)], pair_send.at[g, m], pair_recv.at[g, m], sibling
        )

    def event(g, s):
        if s == 0:
            landed(block(g, 0, True), block_sem(g, 0, True), 0)
        for up in (True, False):
            if s > 0:
                landed(block(g, s, up), block_sem(g, s, up))
            if s < 4:
                hop(g, s, up).start()
        pair(g, s).start()

    for g in range(min(2, NG)):
        swap(g)

    def sq_copy(r):
        return remote(sq.at[0], sq.at[4 - r], sq_send.at[r], sq_recv.at[4 - r], tensor_dev(r))

    for r in range(1, 4):
        sq_copy(r).start()
    event(0, 0)
    swap(2)
    event(1, 0)
    swap(3)
    for r in range(1, 4):
        sq_copy(4 - r).wait_recv()
    factor = lax.rsqrt((sq[0] + sq[1] + sq[2] + sq[3]) / HD + 1e-06) * SCALE
    factor = jnp.transpose(factor)[:, 0:1]
    normed = (q32 * factor * gain[...][None, :]).astype(jnp.bfloat16)
    for h in range(NH):
        qstage[h] = normed[:, h * HEAD : (h + 1) * HEAD]

    def send_query(r, wait=False):
        back = (NY - r) % NY
        to_group(qstage, qbuf.at[back], q_send.at[r], q_recv.at[back], r, wait)

    for r in range(NY):
        send_query(r)
    event(2, 0)
    event(3, 0)
    event(0, 1)
    event(1, 1)
    event(2, 1)

    def send_mixed(g, r, wait=False):
        back = (NY - r) % NY
        to_group(osend.at[r, heads(g)], orecv.at[back, heads(g)], o_send.at[g, r], o_recv.at[g, back], r, wait)
        to_group(ssend.at[r, heads(g)], srecv.at[back, heads(g)], s_send.at[g, r], s_recv.at[g, back], r, wait)

    def lane_sums(x):
        return functools.reduce(jnp.add, [x[:, lo : lo + HEAD] for lo in range(0, x.shape[1], HEAD)])

    def attend(h, part):
        first, count = PARTS[part]
        q = qbuf[:, h].reshape(NY * ROWS, HEAD)
        k = kv[first : first + count, :, h, 0:ROWS, :].reshape(count * 2 * ROWS, HEAD)
        v = kv[first : first + count, :, h, ROWS : 2 * ROWS, :].reshape(count * 2 * ROWS, HEAD)
        scores = lax.dot_general(q, k, CONTRACT_LAST, preferred_element_type=jnp.float32)
        top = jnp.broadcast_to(jnp.max(scores, axis=1, keepdims=True), (NY * ROWS, HEAD))
        if part > 0:
            old = run_top[h]
            top = jnp.maximum(old, top)
            fade = jnp.exp2(old - top)
        expo = jnp.exp2(scores - jnp.concatenate([top] * (2 * count), axis=1))
        total = lane_sums(expo)
        mixed = jnp.dot(expo.astype(jnp.bfloat16), v, preferred_element_type=jnp.float32)
        if part > 0:
            total = run_total[h] * fade + total
            mixed = run_mix[h] * fade + mixed
        if part < len(PARTS) - 1:
            run_top[h] = top
            run_total[h] = total
            run_mix[h] = mixed
            return
        numbers = columns_to_rows(top, jnp.sum(total, axis=1, keepdims=True))
        for r in range(NY):
            rows = slice(r * ROWS, (r + 1) * ROWS)
            osend[r, h] = mixed[rows].astype(jnp.bfloat16)
            ssend[r, h] = numbers[:, rows]

    def sweep(part, events):
        def step(h, carry):
            for g, (first, count) in enumerate(GROUPS):

                @pl.when(h == first)
                def _(g=g):
                    for due in events.get(g, ()):
                        event(*due)
                    if part == 0:
                        pair(g, 0).wait_recv()
                    pair(g, part + 1).wait_recv()

            attend(h, part)
            if part == len(PARTS) - 1:
                for g, (first, count) in enumerate(GROUPS):

                    @pl.when(h == first + count - 1)
                    def _(g=g):
                        for r in (2, 1, 3, 0):
                            send_mixed(g, r)

            return carry

        lax.fori_loop(0, NH, step, 0)

    def combine(g):
        for r in range(NY):
            landed(orecv.at[r, heads(g)], o_recv.at[g, r], r)
            landed(srecv.at[r, heads(g)], s_recv.at[g, r], r)
        first, count = GROUPS[g]
        for h in range(first, first + count):
            tops = [srecv[r, h, 0:1, :] for r in range(NY)]
            top = functools.reduce(jnp.maximum, tops)
            shares = [jnp.exp2(t - top) for t in tops]
            den = sum(shares[r] * srecv[r, h, 1:2, :] for r in range(NY))
            scales = jnp.transpose(jnp.concatenate([share / den for share in shares] * 2, axis=0))
            num = sum(scales[:, r : r + 1] * orecv[r, h].astype(jnp.float32) for r in range(NY))
            attended[:, h * HEAD : (h + 1) * HEAD] = num.astype(jnp.bfloat16)

    def project(first, count, columns):
        rows = slice(first * HEAD, (first + count) * HEAD)
        return jnp.dot(attended[:, rows], weight[rows, columns], preferred_element_type=jnp.float32)

    def project_early():
        def step(b, carry):
            acc[b] = project(0, GROUPS[-1][0], pl.ds(pl.multiple_of(b * COLS, COLS), COLS))
            return carry

        lax.fori_loop(0, 4, step, 0)

    for r in range(NY):
        landed(qbuf.at[r], q_recv.at[r], r)
    sweep(0, {2: [(3, 1)], 3: [(0, 2)]})
    event(1, 2)
    sweep(1, {2: [(2, 2), (3, 2)], 3: [(0, 3)]})
    event(1, 3)
    sweep(2, {2: [(2, 3), (3, 3), (0, 4)], 3: [(1, 4)]})
    sweep(3, {1: [(2, 4), (3, 4)]})
    copies[4].wait()
    combine(0)
    combine(1)
    combine(2)
    project_early()
    combine(3)

    for copy in copies[5:]:
        copy.wait()

    def branch_part(b, part):
        cols = pl.ds(pl.multiple_of(b * COLS + part * PART, PART), PART)
        return acc[b, :, part * PART : (part + 1) * PART] + project(*GROUPS[-1], cols)

    def sib_copy(i, part):
        return remote(tosib.at[i, part], fromsib.at[i, part], sib_send.at[i, part], sib_recv.at[i, part], sibling)

    def x_copy(part):
        return remote(tox.at[part], fromx.at[part], x_send.at[part], x_recv.at[part], across)

    def stage(i, b):
        for part in range(NP):
            tosib[i, part] = branch_part(b, part).astype(jnp.bfloat16)
            sib_copy(i, part).start()

    stage(0, (1 - xl) * 2 + (1 - core))
    for part in range(NP):
        ours = branch_part((1 - xl) * 2 + core, part)
        sib_copy(0, part).wait_recv()
        tox[part] = (ours + fromsib[0, part].astype(jnp.float32)).astype(jnp.bfloat16)
        x_copy(part).start()
    stage(1, xl * 2 + (1 - core))
    for part in range(NP):
        cols = slice(part * PART, (part + 1) * PART)
        branch = branch_part(tensor, part) + params[0, :, cols]
        sib_copy(1, part).wait_recv()
        mine[part] = hidden[:, cols].astype(jnp.float32) + params[1, :, cols] * (
            branch + fromsib[1, part].astype(jnp.float32)
        )

    total = jnp.zeros((ROWS, HEAD), jnp.float32)
    total_sq = jnp.zeros((ROWS, HEAD), jnp.float32)
    for part in range(NP):
        cols = slice(part * PART, (part + 1) * PART)
        x_copy(part).wait_recv()
        value = mine[part] + params[1, :, cols] * fromx[part].astype(jnp.float32)
        summed[:, cols] = value
        for lo in range(0, PART, HEAD):
            piece = value[:, lo : lo + HEAD]
            total = total + piece
            total_sq = total_sq + piece * piece
    keep = pltpu.make_async_copy(summed, summed_hbm, local.at[0])
    keep.start()
    stats[0] = columns_to_rows(
        jnp.sum(total, axis=1, keepdims=True), jnp.sum(total_sq, axis=1, keepdims=True)
    )

    def st_copy(r):
        return remote(stats.at[0], stats.at[4 - r], st_send.at[r], st_recv.at[4 - r], tensor_dev(r))

    for r in range(1, 4):
        st_copy(r).start()

    for g in range(NG):
        swap(g, wait=True)
        for up in (True, False):
            for s in range(4):
                hop(g, s, up).wait_send()
        for m in range(len(shares)):
            pair(g, m).wait_send()
        for r in range(NY):
            send_mixed(g, r, wait=True)
    for r in range(NY):
        send_query(r, wait=True)
    for r in range(1, 4):
        sq_copy(r).wait_send()
    for part in range(NP):
        sib_copy(0, part).wait_send()
        sib_copy(1, part).wait_send()
        x_copy(part).wait_send()

    for r in range(1, 4):
        st_copy(4 - r).wait_recv()
    sums = (stats[0] + stats[1] + stats[2] + stats[3]) / D
    mean = sums[0:1, :]
    moments[...] = jnp.concatenate([mean, lax.rsqrt(sums[1:8, :] - mean * mean + 1e-06)], axis=0)
    keep.wait()
    for r in range(1, 4):
        st_copy(r).wait_send()


def normalise(summed, moments, shift, scale, residual, modulated):
    columns = jnp.transpose(moments[...])
    mean, inv = columns[:, 0:1], columns[:, 1:2]
    my_cols = pl.ds(pl.multiple_of(lax.axis_index("tensor") * COLS, COLS), COLS)
    value = summed[...]
    residual[...] = value.astype(jnp.bfloat16)
    modulated[...] = ((value - mean) * inv * (1.0 + scale[:, my_cols]) + shift[:, my_cols]).astype(jnp.bfloat16)


def body(
    hidden, query, query_gain, stale_keys, stale_values, out_weight, out_bias, residual_gate, norm_shift, norm_scale
):
    bf16, f32 = jnp.bfloat16, jnp.float32
    vmem = pl.BlockSpec(memory_space=pltpu.VMEM)
    hbm = pl.BlockSpec(memory_space=pltpu.HBM)
    dma = pltpu.SemaphoreType.DMA
    row = lambda x: x.reshape(1, -1)
    out = jax.ShapeDtypeStruct((ROWS, COLS), bf16)
    summed, moments = pl.pallas_call(
        kernel,
        out_shape=(jax.ShapeDtypeStruct((ROWS, COLS), f32), jax.ShapeDtypeStruct((8, ROWS), f32)),
        in_specs=[hbm] * 8,
        out_specs=(hbm, vmem),
        scratch_shapes=[
            pltpu.VMEM((ROWS, NH * HEAD), bf16),
            pltpu.VMEM((NH * HEAD,), f32),
            pltpu.VMEM((ROWS, NH * HEAD), bf16),
            pltpu.VMEM((ROWS, NH * HEAD), bf16),
            pltpu.VMEM((NH * HEAD, D), bf16),
            pltpu.VMEM((ROWS, COLS), bf16),
            pltpu.VMEM((2, 1, COLS), f32),
            pltpu.VMEM((NH, 2 * ROWS, HEAD), bf16),
            pltpu.VMEM((NH, ROWS, HEAD), bf16),
            pltpu.VMEM((NZ, 2, NH, 2 * ROWS, HEAD), bf16),
            pltpu.VMEM((NY, NH, ROWS, HEAD), bf16),
            pltpu.VMEM((NY, NH, ROWS, HEAD), bf16),
            pltpu.VMEM((NY, NH, ROWS, HEAD), bf16),
            pltpu.VMEM((NY, NH, 8, ROWS), f32),
            pltpu.VMEM((NY, NH, 8, ROWS), f32),
            pltpu.VMEM((NH, NY * ROWS, HEAD), f32),
            pltpu.VMEM((NH, NY * ROWS, HEAD), f32),
            pltpu.VMEM((NH, NY * ROWS, HEAD), f32),
            pltpu.VMEM((ROWS, NH * HEAD), bf16),
            pltpu.VMEM((4, ROWS, COLS), f32),
            pltpu.VMEM((4, 8, ROWS), f32),
            pltpu.VMEM((4, 8, ROWS), f32),
            pltpu.VMEM((2, NP, ROWS, PART), bf16),
            pltpu.VMEM((2, NP, ROWS, PART), bf16),
            pltpu.VMEM((NP, ROWS, PART), bf16),
            pltpu.VMEM((NP, ROWS, PART), bf16),
            pltpu.VMEM((NP, ROWS, PART), f32),
            pltpu.VMEM((ROWS, COLS), f32),
            dma((NG,)),
            dma((NG, 2, 4)),
            dma((NG, NZ + 1)),
            dma((NG, 5)),
            dma((NG, 5)),
            dma((NY,)),
            dma((NY,)),
        ]
        + [dma((NG, NY))] * 4
        + [dma((4,))] * 4
        + [dma((2, NP))] * 2
        + [dma((NP,))] * 2
        + [dma((8,))],
        compiler_params=pltpu.CompilerParams(
            collective_id=0, has_side_effects=True, vmem_limit_bytes=56 * 2**20
        ),
        name="attention_block",
    )(
        query, query_gain, stale_keys, stale_values, hidden, out_weight,
        row(out_bias), row(residual_gate),
    )
    return pl.pallas_call(
        normalise,
        out_shape=(out, out),
        in_specs=[vmem] * 4,
        out_specs=(vmem, vmem),
        compiler_params=pltpu.CompilerParams(vmem_limit_bytes=56 * 2**20),
        name="normalise",
    )(summed, moments, row(norm_shift), row(norm_scale))


def solution(mesh):
    return jax.shard_map(
        body,
        mesh=mesh,
        in_specs=(
            P("patch", None),
            P("patch", "tensor"),
            P("tensor"),
            P("patch", "tensor"),
            P("patch", "tensor"),
            P("tensor", None),
            P(),
            P(),
            P(),
            P(),
        ),
        out_specs=(P("patch", "tensor"), P("patch", "tensor")),
        check_vma=False,
    )
```

```python
import functools
import math

import jax
import jax.numpy as jnp
from jax import lax
from jax.experimental import pallas as pl
from jax.experimental.pallas import tpu as pltpu
from jax.sharding import PartitionSpec as P

D = 5120
HEAD = 128
HD = 2560
ROWS = 128
NH = 5
GROUPS = ((0, 1), (1, 2), (3, 1), (4, 1))
NG = len(GROUPS)
NZ = 8
NY = 4
PARTS = ((0, 3), (3, 2), (5, 2), (7, 1))
COLS = 1280
PART = 256
NP = COLS // PART
MESH = pl.DeviceIdType.MESH
SCALE = HEAD**-0.5 * math.log2(math.e)
CONTRACT_LAST = (((1,), (1,)), ((), ()))


def remote(src, dst, send, recv, device):
    return pltpu.make_async_remote_copy(
        src_ref=src, dst_ref=dst, send_sem=send, recv_sem=recv, device_id=device, device_id_type=MESH
    )


def columns_to_rows(first, second):
    n = first.shape[0]
    lane = lax.broadcasted_iota(jnp.int32, (n, HEAD), 1)
    return jnp.transpose(jnp.where(lane == 0, first, second))[0:8]


def kernel(
    query_hbm, gain_hbm, keys_hbm, values_hbm, hidden_hbm, weight_hbm, bias_hbm, gate_hbm,
    summed_hbm, moments,
    query, gain, keys, values, weight, hidden, params,
    kvstage, qstage, kv, qbuf, osend, orecv, ssend, srecv, run_mix, run_top, run_total, attended, acc,
    sq, stats, tosib, fromsib, tox, fromx, mine, summed,
    swap_send, kv_send, kv_recv, pair_send, pair_recv, q_send, q_recv, o_send, o_recv, s_send, s_recv, sq_send, sq_recv,
    st_send, st_recv, sib_send, sib_recv, x_send, x_recv, local,
):
    patch = lax.axis_index("patch")
    tensor = lax.axis_index("tensor")
    y, z, xh = patch // 16, (patch // 2) % 8, patch % 2
    xl, core = tensor // 2, tensor % 2
    straight = xh == core

    def z_dev(step):
        return {"patch": y * 16 + ((z + step + NZ) % NZ) * 2 + xh, "tensor": tensor}

    def group_dev(r):
        return {"patch": ((y + r) % NY) * 16 + z * 2 + core, "tensor": xl * 2 + xh}

    def tensor_dev(r):
        return {"patch": patch, "tensor": (tensor + r) % 4}

    sibling = {"patch": patch, "tensor": xl * 2 + (1 - core)}
    across = {"patch": patch, "tensor": (1 - xl) * 2 + core}

    barrier = pltpu.get_barrier_semaphore()
    partners = [z_dev(1), z_dev(-1)] + [group_dev(r) for r in range(1, NY)] + [tensor_dev(r) for r in range(1, 4)]
    for device in partners:
        pl.semaphore_signal(barrier, inc=1, device_id=device, device_id_type=MESH)

    @pl.when(jnp.logical_not(straight))
    def _():
        pl.semaphore_signal(barrier, inc=1, device_id=group_dev(0), device_id_type=MESH)

    my_cols = pl.ds(pl.multiple_of(tensor * COLS, COLS), COLS)
    early = [(keys_hbm, keys), (values_hbm, values), (query_hbm, query), (gain_hbm, gain)]
    late = [(weight_hbm, weight), (hidden_hbm.at[:, my_cols], hidden)]
    late += [(ref.at[:, my_cols], params.at[i]) for i, ref in enumerate((bias_hbm, gate_hbm))]
    copies = [pltpu.make_async_copy(src, dst, local.at[i]) for i, (src, dst) in enumerate(early + late)]
    for copy in copies:
        copy.start()

    copies[0].wait()
    copies[1].wait()
    for h in range(NH):
        cols = slice(h * HEAD, (h + 1) * HEAD)
        kvstage[h, 0:ROWS, :] = keys[:, cols]
        kvstage[h, ROWS:, :] = values[:, cols]

    copies[2].wait()
    copies[3].wait()
    q32 = query[...].astype(jnp.float32)
    squares = jnp.sum(q32 * q32, axis=1, keepdims=True)
    sq[0] = columns_to_rows(squares, squares)

    @pl.when(straight)
    def _():
        pl.semaphore_wait(barrier, len(partners))

    @pl.when(jnp.logical_not(straight))
    def _():
        pl.semaphore_wait(barrier, len(partners) + 1)

    def to_group(src, dst, send, recv, r, wait=False):
        copy = remote(src, dst, send, recv, group_dev(r))
        act = copy.wait_send if wait else copy.start
        if r > 0:
            act()
            return
        pl.when(jnp.logical_not(straight))(act)
        if not wait:

            @pl.when(straight)
            def _():
                dst[...] = src[...]

    def landed(ref, recv, r=1):
        wait = remote(ref, ref, swap_send.at[0], recv, z_dev(1)).wait_recv
        if r > 0:
            wait()
        else:
            pl.when(jnp.logical_not(straight))(wait)

    def heads(g):
        return pl.ds(*GROUPS[g])

    def swap(g, wait=False):
        to_group(kvstage.at[heads(g)], kv.at[0, 0, heads(g)], swap_send.at[g], kv_recv.at[g, 0], 0, wait)

    def place(s, up):
        return 0 if s == 0 else 2 * s - 1 if up or s == 4 else 2 * s

    def block(g, s, up):
        if s == 4:
            return kv.at[7, 0, heads(g), pl.ds(0 if up else ROWS, ROWS)]
        return kv.at[place(s, up), 0, heads(g)]

    def block_sem(g, s, up):
        return kv_recv.at[g, 8 if s == 4 and not up else place(s, up)]

    def hop(g, s, up):
        src = block(g, s, up)
        if s == 3:
            src = kv.at[place(s, up), 0, heads(g), pl.ds(0 if up else ROWS, ROWS)]
        return remote(
            src, block(g, s + 1, up), kv_send.at[g, int(up), s], block_sem(g, s + 1, up), z_dev(1 if up else -1)
        )


    def pair(g, m):
        places = pl.ds(*PARTS[m])
        return remote(
            kv.at[places, 0, heads(g)], kv.at[places, 1, heads(g)], pair_send.at[g, m], pair_recv.at[g, m], sibling
        )

    def event(g, s):
        if s == 0:
            landed(block(g, 0, True), block_sem(g, 0, True), 0)
        for up in (True, False):
            if s > 0:
                landed(block(g, s, up), block_sem(g, s, up))
            if s < 4:
                hop(g, s, up).start()
        if s > 0:
            pair(g, s - 1).start()

    for g in range(min(2, NG)):
        swap(g)

    def sq_copy(r):
        return remote(sq.at[0], sq.at[4 - r], sq_send.at[r], sq_recv.at[4 - r], tensor_dev(r))

    for r in range(1, 4):
        sq_copy(r).start()
    event(0, 0)
    swap(2)
    event(1, 0)
    swap(3)
    for g in range(2, NG):
        event(g, 0)
    event(0, 1)
    for r in range(1, 4):
        sq_copy(4 - r).wait_recv()
    factor = lax.rsqrt((sq[0] + sq[1] + sq[2] + sq[3]) / HD + 1e-06) * SCALE
    factor = jnp.transpose(factor)[:, 0:1]
    normed = (q32 * factor * gain[...][None, :]).astype(jnp.bfloat16)
    for h in range(NH):
        qstage[h] = normed[:, h * HEAD : (h + 1) * HEAD]

    def send_query(r, wait=False):
        back = (NY - r) % NY
        to_group(qstage, qbuf.at[back], q_send.at[r], q_recv.at[back], r, wait)

    for r in range(NY):
        send_query(r)
    for g in range(1, NG):
        event(g, 1)
    event(0, 2)

    def send_mixed(g, r, wait=False):
        back = (NY - r) % NY
        to_group(osend.at[r, heads(g)], orecv.at[back, heads(g)], o_send.at[g, r], o_recv.at[g, back], r, wait)
        to_group(ssend.at[r, heads(g)], srecv.at[back, heads(g)], s_send.at[g, r], s_recv.at[g, back], r, wait)

    def lane_sums(x):
        return functools.reduce(jnp.add, [x[:, lo : lo + HEAD] for lo in range(0, x.shape[1], HEAD)])

    def attend(h, part):
        first, count = PARTS[part]
        q = qbuf[:, h].reshape(NY * ROWS, HEAD)
        k = kv[first : first + count, :, h, 0:ROWS, :].reshape(count * 2 * ROWS, HEAD)
        v = kv[first : first + count, :, h, ROWS : 2 * ROWS, :].reshape(count * 2 * ROWS, HEAD)
        scores = lax.dot_general(q, k, CONTRACT_LAST, preferred_element_type=jnp.float32)
        top = jnp.broadcast_to(jnp.max(scores, axis=1, keepdims=True), (NY * ROWS, HEAD))
        if part > 0:
            old = run_top[h]
            top = jnp.maximum(old, top)
            fade = jnp.exp2(old - top)
        expo = jnp.exp2(scores - jnp.concatenate([top] * (2 * count), axis=1))
        total = lane_sums(expo)
        mixed = jnp.dot(expo.astype(jnp.bfloat16), v, preferred_element_type=jnp.float32)
        if part > 0:
            total = run_total[h] * fade + total
            mixed = run_mix[h] * fade + mixed
        if part < len(PARTS) - 1:
            run_top[h] = top
            run_total[h] = total
            run_mix[h] = mixed
            return
        numbers = columns_to_rows(top, jnp.sum(total, axis=1, keepdims=True))
        for r in range(NY):
            rows = slice(r * ROWS, (r + 1) * ROWS)
            osend[r, h] = mixed[rows].astype(jnp.bfloat16)
            ssend[r, h] = numbers[:, rows]

    def sweep(part, events):
        def step(h, carry):
            for g, (first, count) in enumerate(GROUPS):

                @pl.when(h == first)
                def _(g=g):
                    for due in events.get(g, ()):
                        event(*due)
                    pair(g, part).wait_recv()

            attend(h, part)
            if part == len(PARTS) - 1:
                for g, (first, count) in enumerate(GROUPS):

                    @pl.when(h == first + count - 1)
                    def _(g=g):
                        for r in (2, 1, 3, 0):
                            send_mixed(g, r)

            return carry

        lax.fori_loop(0, NH, step, 0)

    def combine(g):
        for r in range(NY):
            landed(orecv.at[r, heads(g)], o_recv.at[g, r], r)
            landed(srecv.at[r, heads(g)], s_recv.at[g, r], r)
        first, count = GROUPS[g]
        for h in range(first, first + count):
            tops = [srecv[r, h, 0:1, :] for r in range(NY)]
            top = functools.reduce(jnp.maximum, tops)
            shares = [jnp.exp2(t - top) for t in tops]
            den = sum(shares[r] * srecv[r, h, 1:2, :] for r in range(NY))
            scales = jnp.transpose(jnp.concatenate([share / den for share in shares] * 2, axis=0))
            num = sum(scales[:, r : r + 1] * orecv[r, h].astype(jnp.float32) for r in range(NY))
            attended[:, h * HEAD : (h + 1) * HEAD] = num.astype(jnp.bfloat16)

    def project(first, count, columns):
        rows = slice(first * HEAD, (first + count) * HEAD)
        return jnp.dot(attended[:, rows], weight[rows, columns], preferred_element_type=jnp.float32)

    def project_early():
        def step(b, carry):
            acc[b] = project(0, GROUPS[-1][0], pl.ds(pl.multiple_of(b * COLS, COLS), COLS))
            return carry

        lax.fori_loop(0, 4, step, 0)

    for r in range(NY):
        landed(qbuf.at[r], q_recv.at[r], r)
    sweep(0, {g: [(g, 2)] for g in range(1, NG)})
    sweep(1, {g: [(g, 3)] for g in range(NG)})
    sweep(2, {g: [(g, 4)] for g in range(NG)})
    sweep(3, {})
    copies[4].wait()
    for g in range(NG - 1):
        combine(g)
    project_early()
    combine(NG - 1)

    for copy in copies[5:]:
        copy.wait()

    def branch_part(b, part):
        cols = pl.ds(pl.multiple_of(b * COLS + part * PART, PART), PART)
        return acc[b, :, part * PART : (part + 1) * PART] + project(*GROUPS[-1], cols)

    def sib_copy(i, part):
        return remote(tosib.at[i, part], fromsib.at[i, part], sib_send.at[i, part], sib_recv.at[i, part], sibling)

    def x_copy(part):
        return remote(tox.at[part], fromx.at[part], x_send.at[part], x_recv.at[part], across)

    def stage(i, b):
        for part in range(NP):
            tosib[i, part] = branch_part(b, part).astype(jnp.bfloat16)
            sib_copy(i, part).start()

    stage(0, (1 - xl) * 2 + (1 - core))
    for part in range(NP):
        ours = branch_part((1 - xl) * 2 + core, part)
        sib_copy(0, part).wait_recv()
        tox[part] = (ours + fromsib[0, part].astype(jnp.float32)).astype(jnp.bfloat16)
        x_copy(part).start()
    stage(1, xl * 2 + (1 - core))
    for part in range(NP):
        cols = slice(part * PART, (part + 1) * PART)
        branch = branch_part(tensor, part) + params[0, :, cols]
        sib_copy(1, part).wait_recv()
        mine[part] = hidden[:, cols].astype(jnp.float32) + params[1, :, cols] * (
            branch + fromsib[1, part].astype(jnp.float32)
        )

    total = jnp.zeros((ROWS, HEAD), jnp.float32)
    total_sq = jnp.zeros((ROWS, HEAD), jnp.float32)
    for part in range(NP):
        cols = slice(part * PART, (part + 1) * PART)
        x_copy(part).wait_recv()
        value = mine[part] + params[1, :, cols] * fromx[part].astype(jnp.float32)
        summed[:, cols] = value
        for lo in range(0, PART, HEAD):
            piece = value[:, lo : lo + HEAD]
            total = total + piece
            total_sq = total_sq + piece * piece
    keep = pltpu.make_async_copy(summed, summed_hbm, local.at[0])
    keep.start()
    stats[0] = columns_to_rows(
        jnp.sum(total, axis=1, keepdims=True), jnp.sum(total_sq, axis=1, keepdims=True)
    )

    def st_copy(r):
        return remote(stats.at[0], stats.at[4 - r], st_send.at[r], st_recv.at[4 - r], tensor_dev(r))

    for r in range(1, 4):
        st_copy(r).start()

    for g in range(NG):
        swap(g, wait=True)
        for up in (True, False):
            for s in range(4):
                hop(g, s, up).wait_send()
        for m in range(len(PARTS)):
            pair(g, m).wait_send()
        for r in range(NY):
            send_mixed(g, r, wait=True)
    for r in range(NY):
        send_query(r, wait=True)
    for r in range(1, 4):
        sq_copy(r).wait_send()
    for part in range(NP):
        sib_copy(0, part).wait_send()
        sib_copy(1, part).wait_send()
        x_copy(part).wait_send()

    for r in range(1, 4):
        st_copy(4 - r).wait_recv()
    sums = (stats[0] + stats[1] + stats[2] + stats[3]) / D
    mean = sums[0:1, :]
    moments[...] = jnp.concatenate([mean, lax.rsqrt(sums[1:8, :] - mean * mean + 1e-06)], axis=0)
    keep.wait()
    for r in range(1, 4):
        st_copy(r).wait_send()


def normalise(summed, moments, shift, scale, residual, modulated):
    columns = jnp.transpose(moments[...])
    mean, inv = columns[:, 0:1], columns[:, 1:2]
    my_cols = pl.ds(pl.multiple_of(lax.axis_index("tensor") * COLS, COLS), COLS)
    value = summed[...]
    residual[...] = value.astype(jnp.bfloat16)
    modulated[...] = ((value - mean) * inv * (1.0 + scale[:, my_cols]) + shift[:, my_cols]).astype(jnp.bfloat16)


def body(
    hidden, query, query_gain, stale_keys, stale_values, out_weight, out_bias, residual_gate, norm_shift, norm_scale
):
    bf16, f32 = jnp.bfloat16, jnp.float32
    vmem = pl.BlockSpec(memory_space=pltpu.VMEM)
    hbm = pl.BlockSpec(memory_space=pltpu.HBM)
    dma = pltpu.SemaphoreType.DMA
    row = lambda x: x.reshape(1, -1)
    out = jax.ShapeDtypeStruct((ROWS, COLS), bf16)
    summed, moments = pl.pallas_call(
        kernel,
        out_shape=(jax.ShapeDtypeStruct((ROWS, COLS), f32), jax.ShapeDtypeStruct((8, ROWS), f32)),
        in_specs=[hbm] * 8,
        out_specs=(hbm, vmem),
        scratch_shapes=[
            pltpu.VMEM((ROWS, NH * HEAD), bf16),
            pltpu.VMEM((NH * HEAD,), f32),
            pltpu.VMEM((ROWS, NH * HEAD), bf16),
            pltpu.VMEM((ROWS, NH * HEAD), bf16),
            pltpu.VMEM((NH * HEAD, D), bf16),
            pltpu.VMEM((ROWS, COLS), bf16),
            pltpu.VMEM((2, 1, COLS), f32),
            pltpu.VMEM((NH, 2 * ROWS, HEAD), bf16),
            pltpu.VMEM((NH, ROWS, HEAD), bf16),
            pltpu.VMEM((NZ, 2, NH, 2 * ROWS, HEAD), bf16),
            pltpu.VMEM((NY, NH, ROWS, HEAD), bf16),
            pltpu.VMEM((NY, NH, ROWS, HEAD), bf16),
            pltpu.VMEM((NY, NH, ROWS, HEAD), bf16),
            pltpu.VMEM((NY, NH, 8, ROWS), f32),
            pltpu.VMEM((NY, NH, 8, ROWS), f32),
            pltpu.VMEM((NH, NY * ROWS, HEAD), f32),
            pltpu.VMEM((NH, NY * ROWS, HEAD), f32),
            pltpu.VMEM((NH, NY * ROWS, HEAD), f32),
            pltpu.VMEM((ROWS, NH * HEAD), bf16),
            pltpu.VMEM((4, ROWS, COLS), f32),
            pltpu.VMEM((4, 8, ROWS), f32),
            pltpu.VMEM((4, 8, ROWS), f32),
            pltpu.VMEM((2, NP, ROWS, PART), bf16),
            pltpu.VMEM((2, NP, ROWS, PART), bf16),
            pltpu.VMEM((NP, ROWS, PART), bf16),
            pltpu.VMEM((NP, ROWS, PART), bf16),
            pltpu.VMEM((NP, ROWS, PART), f32),
            pltpu.VMEM((ROWS, COLS), f32),
            dma((NG,)),
            dma((NG, 2, 4)),
            dma((NG, NZ + 1)),
            dma((NG, 4)),
            dma((NG, 4)),
            dma((NY,)),
            dma((NY,)),
        ]
        + [dma((NG, NY))] * 4
        + [dma((4,))] * 4
        + [dma((2, NP))] * 2
        + [dma((NP,))] * 2
        + [dma((8,))],
        compiler_params=pltpu.CompilerParams(
            collective_id=0, has_side_effects=True, vmem_limit_bytes=56 * 2**20
        ),
        name="attention_block",
    )(
        query, query_gain, stale_keys, stale_values, hidden, out_weight,
        row(out_bias), row(residual_gate),
    )
    return pl.pallas_call(
        normalise,
        out_shape=(out, out),
        in_specs=[vmem] * 4,
        out_specs=(vmem, vmem),
        compiler_params=pltpu.CompilerParams(vmem_limit_bytes=56 * 2**20),
        name="normalise",
    )(summed, moments, row(norm_shift), row(norm_scale))


def solution(mesh):
    return jax.shard_map(
        body,
        mesh=mesh,
        in_specs=(
            P("patch", None),
            P("patch", "tensor"),
            P("tensor"),
            P("patch", "tensor"),
            P("patch", "tensor"),
            P("tensor", None),
            P(),
            P(),
            P(),
            P(),
        ),
        out_specs=(P("patch", "tensor"), P("patch", "tensor")),
        check_vma=False,
    )
```

```python
import functools
import math

import jax
import jax.numpy as jnp
from jax import lax
from jax.experimental import pallas as pl
from jax.experimental.pallas import tpu as pltpu
from jax.sharding import PartitionSpec as P

D = 5120
HEAD = 128
HD = 2560
ROWS = 128
NH = 5
GROUPS = ((0, 1), (1, 2), (3, 1), (4, 1))
NG = len(GROUPS)
NZ = 8
NY = 4
PARTS = ((0, 3), (3, 2), (5, 2), (7, 1))
COLS = 1280
PART = 256
NP = COLS // PART
MESH = pl.DeviceIdType.MESH
SCALE = HEAD**-0.5 * math.log2(math.e)
CONTRACT_LAST = (((1,), (1,)), ((), ()))


def remote(src, dst, send, recv, device):
    return pltpu.make_async_remote_copy(
        src_ref=src, dst_ref=dst, send_sem=send, recv_sem=recv, device_id=device, device_id_type=MESH
    )


def columns_to_rows(first, second):
    n = first.shape[0]
    lane = lax.broadcasted_iota(jnp.int32, (n, HEAD), 1)
    return jnp.transpose(jnp.where(lane == 0, first, second))[0:8]


def kernel(
    query_hbm, gain_hbm, keys_hbm, values_hbm, hidden_hbm, weight_hbm, bias_hbm, gate_hbm,
    summed_hbm, moments,
    query, gain, keys, values, weight, hidden, params,
    kvstage, qstage, kv, qbuf, osend, orecv, ssend, srecv, run_mix, run_top, run_total, attended, acc,
    sq, stats, tosib, fromsib, tox, fromx, mine, summed,
    swap_send, kv_send, kv_recv, pair_send, pair_recv, q_send, q_recv, o_send, o_recv, s_send, s_recv, sq_send, sq_recv,
    st_send, st_recv, sib_send, sib_recv, x_send, x_recv, local,
):
    patch = lax.axis_index("patch")
    tensor = lax.axis_index("tensor")
    y, z, xh = patch // 16, (patch // 2) % 8, patch % 2
    xl, core = tensor // 2, tensor % 2
    straight = xh == core

    def z_dev(step):
        return {"patch": y * 16 + ((z + step + NZ) % NZ) * 2 + xh, "tensor": tensor}

    def group_dev(r):
        return {"patch": ((y + r) % NY) * 16 + z * 2 + core, "tensor": xl * 2 + xh}

    def tensor_dev(r):
        return {"patch": patch, "tensor": (tensor + r) % 4}

    sibling = {"patch": patch, "tensor": xl * 2 + (1 - core)}
    across = {"patch": patch, "tensor": (1 - xl) * 2 + core}

    barrier = pltpu.get_barrier_semaphore()
    partners = [z_dev(1), z_dev(-1)] + [group_dev(r) for r in range(1, NY)] + [tensor_dev(r) for r in range(1, 4)]
    for device in partners:
        pl.semaphore_signal(barrier, inc=1, device_id=device, device_id_type=MESH)

    @pl.when(jnp.logical_not(straight))
    def _():
        pl.semaphore_signal(barrier, inc=1, device_id=group_dev(0), device_id_type=MESH)

    my_cols = pl.ds(pl.multiple_of(tensor * COLS, COLS), COLS)
    early = [(keys_hbm, keys), (values_hbm, values), (query_hbm, query), (gain_hbm, gain)]
    late = [(weight_hbm, weight), (hidden_hbm.at[:, my_cols], hidden)]
    late += [(ref.at[:, my_cols], params.at[i]) for i, ref in enumerate((bias_hbm, gate_hbm))]
    copies = [pltpu.make_async_copy(src, dst, local.at[i]) for i, (src, dst) in enumerate(early + late)]
    for copy in copies:
        copy.start()

    copies[0].wait()
    copies[1].wait()
    for h in range(NH):
        cols = slice(h * HEAD, (h + 1) * HEAD)
        kvstage[h, 0:ROWS, :] = keys[:, cols]
        kvstage[h, ROWS:, :] = values[:, cols]

    copies[2].wait()
    copies[3].wait()
    q32 = query[...].astype(jnp.float32)
    squares = jnp.sum(q32 * q32, axis=1, keepdims=True)
    sq[0] = columns_to_rows(squares, squares)

    @pl.when(straight)
    def _():
        pl.semaphore_wait(barrier, len(partners))

    @pl.when(jnp.logical_not(straight))
    def _():
        pl.semaphore_wait(barrier, len(partners) + 1)

    def to_group(src, dst, send, recv, r, wait=False):
        copy = remote(src, dst, send, recv, group_dev(r))
        act = copy.wait_send if wait else copy.start
        if r > 0:
            act()
            return
        pl.when(jnp.logical_not(straight))(act)
        if not wait:

            @pl.when(straight)
            def _():
                dst[...] = src[...]

    def landed(ref, recv, r=1):
        wait = remote(ref, ref, swap_send.at[0], recv, z_dev(1)).wait_recv
        if r > 0:
            wait()
        else:
            pl.when(jnp.logical_not(straight))(wait)

    def heads(g):
        return pl.ds(*GROUPS[g])

    def swap(g, wait=False):
        to_group(kvstage.at[heads(g)], kv.at[0, 0, heads(g)], swap_send.at[g], kv_recv.at[g, 0], 0, wait)

    def place(s, up):
        return 0 if s == 0 else 2 * s - 1 if up or s == 4 else 2 * s

    def block(g, s, up):
        if s == 4:
            return kv.at[7, 0, heads(g), pl.ds(0 if up else ROWS, ROWS)]
        return kv.at[place(s, up), 0, heads(g)]

    def block_sem(g, s, up):
        return kv_recv.at[g, 8 if s == 4 and not up else place(s, up)]

    def hop(g, s, up):
        src = block(g, s, up)
        if s == 3:
            src = kv.at[place(s, up), 0, heads(g), pl.ds(0 if up else ROWS, ROWS)]
        return remote(
            src, block(g, s + 1, up), kv_send.at[g, int(up), s], block_sem(g, s + 1, up), z_dev(1 if up else -1)
        )


    def pair(g, m):
        places = pl.ds(*PARTS[m])
        return remote(
            kv.at[places, 0, heads(g)], kv.at[places, 1, heads(g)], pair_send.at[g, m], pair_recv.at[g, m], sibling
        )

    def event(g, s):
        if s == 0:
            landed(block(g, 0, True), block_sem(g, 0, True), 0)
        for up in (True, False):
            if s > 0:
                landed(block(g, s, up), block_sem(g, s, up))
            if s < 4:
                hop(g, s, up).start()
        if s > 0:
            pair(g, s - 1).start()

    for g in range(min(2, NG)):
        swap(g)

    def sq_copy(r):
        return remote(sq.at[0], sq.at[4 - r], sq_send.at[r], sq_recv.at[4 - r], tensor_dev(r))

    for r in range(1, 4):
        sq_copy(r).start()
    event(0, 0)
    swap(2)
    event(1, 0)
    swap(3)
    for r in range(1, 4):
        sq_copy(4 - r).wait_recv()
    factor = lax.rsqrt((sq[0] + sq[1] + sq[2] + sq[3]) / HD + 1e-06) * SCALE
    factor = jnp.transpose(factor)[:, 0:1]
    normed = (q32 * factor * gain[...][None, :]).astype(jnp.bfloat16)
    for h in range(NH):
        qstage[h] = normed[:, h * HEAD : (h + 1) * HEAD]

    def send_query(r, wait=False):
        back = (NY - r) % NY
        to_group(qstage, qbuf.at[back], q_send.at[r], q_recv.at[back], r, wait)

    for r in range(NY):
        send_query(r)
    for g in range(2, NG):
        event(g, 0)
    for g in range(NG):
        event(g, 1)
    for g in range(2):
        event(g, 2)

    def send_mixed(g, r, wait=False):
        back = (NY - r) % NY
        to_group(osend.at[r, heads(g)], orecv.at[back, heads(g)], o_send.at[g, r], o_recv.at[g, back], r, wait)
        to_group(ssend.at[r, heads(g)], srecv.at[back, heads(g)], s_send.at[g, r], s_recv.at[g, back], r, wait)

    def lane_sums(x):
        return functools.reduce(jnp.add, [x[:, lo : lo + HEAD] for lo in range(0, x.shape[1], HEAD)])

    def attend(h, part):
        first, count = PARTS[part]
        q = qbuf[:, h].reshape(NY * ROWS, HEAD)
        k = kv[first : first + count, :, h, 0:ROWS, :].reshape(count * 2 * ROWS, HEAD)
        v = kv[first : first + count, :, h, ROWS : 2 * ROWS, :].reshape(count * 2 * ROWS, HEAD)
        scores = lax.dot_general(q, k, CONTRACT_LAST, preferred_element_type=jnp.float32)
        top = jnp.broadcast_to(jnp.max(scores, axis=1, keepdims=True), (NY * ROWS, HEAD))
        if part > 0:
            old = run_top[h]
            top = jnp.maximum(old, top)
            fade = jnp.exp2(old - top)
        expo = jnp.exp2(scores - jnp.concatenate([top] * (2 * count), axis=1))
        total = lane_sums(expo)
        mixed = jnp.dot(expo.astype(jnp.bfloat16), v, preferred_element_type=jnp.float32)
        if part > 0:
            total = run_total[h] * fade + total
            mixed = run_mix[h] * fade + mixed
        if part < len(PARTS) - 1:
            run_top[h] = top
            run_total[h] = total
            run_mix[h] = mixed
            return
        numbers = columns_to_rows(top, jnp.sum(total, axis=1, keepdims=True))
        for r in range(NY):
            rows = slice(r * ROWS, (r + 1) * ROWS)
            osend[r, h] = mixed[rows].astype(jnp.bfloat16)
            ssend[r, h] = numbers[:, rows]

    def sweep(part, events):
        def step(h, carry):
            for g, (first, count) in enumerate(GROUPS):

                @pl.when(h == first)
                def _(g=g):
                    for due in events.get(g, ()):
                        event(*due)
                    pair(g, part).wait_recv()

            attend(h, part)
            if part == len(PARTS) - 1:
                for g, (first, count) in enumerate(GROUPS):

                    @pl.when(h == first + count - 1)
                    def _(g=g):
                        for r in (2, 1, 3, 0):
                            send_mixed(g, r)

            return carry

        lax.fori_loop(0, NH, step, 0)

    def combine(g):
        for r in range(NY):
            landed(orecv.at[r, heads(g)], o_recv.at[g, r], r)
            landed(srecv.at[r, heads(g)], s_recv.at[g, r], r)
        first, count = GROUPS[g]
        for h in range(first, first + count):
            tops = [srecv[r, h, 0:1, :] for r in range(NY)]
            top = functools.reduce(jnp.maximum, tops)
            shares = [jnp.exp2(t - top) for t in tops]
            den = sum(shares[r] * srecv[r, h, 1:2, :] for r in range(NY))
            scales = jnp.transpose(jnp.concatenate([share / den for share in shares] * 2, axis=0))
            num = sum(scales[:, r : r + 1] * orecv[r, h].astype(jnp.float32) for r in range(NY))
            attended[:, h * HEAD : (h + 1) * HEAD] = num.astype(jnp.bfloat16)

    def project(first, count, columns):
        rows = slice(first * HEAD, (first + count) * HEAD)
        return jnp.dot(attended[:, rows], weight[rows, columns], preferred_element_type=jnp.float32)

    def project_early():
        def step(b, carry):
            acc[b] = project(0, GROUPS[-1][0], pl.ds(pl.multiple_of(b * COLS, COLS), COLS))
            return carry

        lax.fori_loop(0, 4, step, 0)

    for r in range(NY):
        landed(qbuf.at[r], q_recv.at[r], r)
    sweep(0, {2: [(2, 2)], 3: [(3, 2)]})
    sweep(1, {0: [(0, 3)], 1: [(1, 3)], 2: [(2, 3)], 3: [(3, 3)]})
    sweep(2, {0: [(0, 4)], 1: [(1, 4)], 2: [(2, 4)], 3: [(3, 4)]})
    sweep(3, {})
    copies[4].wait()
    for g in range(NG - 1):
        combine(g)
    project_early()
    combine(NG - 1)

    for copy in copies[5:]:
        copy.wait()

    def branch_part(b, part):
        cols = pl.ds(pl.multiple_of(b * COLS + part * PART, PART), PART)
        return acc[b, :, part * PART : (part + 1) * PART] + project(*GROUPS[-1], cols)

    def sib_copy(i, part):
        return remote(tosib.at[i, part], fromsib.at[i, part], sib_send.at[i, part], sib_recv.at[i, part], sibling)

    def x_copy(part):
        return remote(tox.at[part], fromx.at[part], x_send.at[part], x_recv.at[part], across)

    def stage(i, b):
        for part in range(NP):
            tosib[i, part] = branch_part(b, part).astype(jnp.bfloat16)
            sib_copy(i, part).start()

    stage(0, (1 - xl) * 2 + (1 - core))
    for part in range(NP):
        ours = branch_part((1 - xl) * 2 + core, part)
        sib_copy(0, part).wait_recv()
        tox[part] = (ours + fromsib[0, part].astype(jnp.float32)).astype(jnp.bfloat16)
        x_copy(part).start()
    stage(1, xl * 2 + (1 - core))
    for part in range(NP):
        cols = slice(part * PART, (part + 1) * PART)
        branch = branch_part(tensor, part) + params[0, :, cols]
        sib_copy(1, part).wait_recv()
        mine[part] = hidden[:, cols].astype(jnp.float32) + params[1, :, cols] * (
            branch + fromsib[1, part].astype(jnp.float32)
        )

    total = jnp.zeros((ROWS, HEAD), jnp.float32)
    total_sq = jnp.zeros((ROWS, HEAD), jnp.float32)
    for part in range(NP):
        cols = slice(part * PART, (part + 1) * PART)
        x_copy(part).wait_recv()
        value = mine[part] + params[1, :, cols] * fromx[part].astype(jnp.float32)
        summed[:, cols] = value
        for lo in range(0, PART, HEAD):
            piece = value[:, lo : lo + HEAD]
            total = total + piece
            total_sq = total_sq + piece * piece
    keep = pltpu.make_async_copy(summed, summed_hbm, local.at[0])
    keep.start()
    stats[0] = columns_to_rows(
        jnp.sum(total, axis=1, keepdims=True), jnp.sum(total_sq, axis=1, keepdims=True)
    )

    def st_copy(r):
        return remote(stats.at[0], stats.at[4 - r], st_send.at[r], st_recv.at[4 - r], tensor_dev(r))

    for r in range(1, 4):
        st_copy(r).start()

    for g in range(NG):
        swap(g, wait=True)
        for up in (True, False):
            for s in range(4):
                hop(g, s, up).wait_send()
        for m in range(len(PARTS)):
            pair(g, m).wait_send()
        for r in range(NY):
            send_mixed(g, r, wait=True)
    for r in range(NY):
        send_query(r, wait=True)
    for r in range(1, 4):
        sq_copy(r).wait_send()
    for part in range(NP):
        sib_copy(0, part).wait_send()
        sib_copy(1, part).wait_send()
        x_copy(part).wait_send()

    for r in range(1, 4):
        st_copy(4 - r).wait_recv()
    sums = (stats[0] + stats[1] + stats[2] + stats[3]) / D
    mean = sums[0:1, :]
    moments[...] = jnp.concatenate([mean, lax.rsqrt(sums[1:8, :] - mean * mean + 1e-06)], axis=0)
    keep.wait()
    for r in range(1, 4):
        st_copy(r).wait_send()


def normalise(summed, moments, shift, scale, residual, modulated):
    columns = jnp.transpose(moments[...])
    mean, inv = columns[:, 0:1], columns[:, 1:2]
    my_cols = pl.ds(pl.multiple_of(lax.axis_index("tensor") * COLS, COLS), COLS)
    value = summed[...]
    residual[...] = value.astype(jnp.bfloat16)
    modulated[...] = ((value - mean) * inv * (1.0 + scale[:, my_cols]) + shift[:, my_cols]).astype(jnp.bfloat16)


def body(
    hidden, query, query_gain, stale_keys, stale_values, out_weight, out_bias, residual_gate, norm_shift, norm_scale
):
    bf16, f32 = jnp.bfloat16, jnp.float32
    vmem = pl.BlockSpec(memory_space=pltpu.VMEM)
    hbm = pl.BlockSpec(memory_space=pltpu.HBM)
    dma = pltpu.SemaphoreType.DMA
    row = lambda x: x.reshape(1, -1)
    out = jax.ShapeDtypeStruct((ROWS, COLS), bf16)
    summed, moments = pl.pallas_call(
        kernel,
        out_shape=(jax.ShapeDtypeStruct((ROWS, COLS), f32), jax.ShapeDtypeStruct((8, ROWS), f32)),
        in_specs=[hbm] * 8,
        out_specs=(hbm, vmem),
        scratch_shapes=[
            pltpu.VMEM((ROWS, NH * HEAD), bf16),
            pltpu.VMEM((NH * HEAD,), f32),
            pltpu.VMEM((ROWS, NH * HEAD), bf16),
            pltpu.VMEM((ROWS, NH * HEAD), bf16),
            pltpu.VMEM((NH * HEAD, D), bf16),
            pltpu.VMEM((ROWS, COLS), bf16),
            pltpu.VMEM((2, 1, COLS), f32),
            pltpu.VMEM((NH, 2 * ROWS, HEAD), bf16),
            pltpu.VMEM((NH, ROWS, HEAD), bf16),
            pltpu.VMEM((NZ, 2, NH, 2 * ROWS, HEAD), bf16),
            pltpu.VMEM((NY, NH, ROWS, HEAD), bf16),
            pltpu.VMEM((NY, NH, ROWS, HEAD), bf16),
            pltpu.VMEM((NY, NH, ROWS, HEAD), bf16),
            pltpu.VMEM((NY, NH, 8, ROWS), f32),
            pltpu.VMEM((NY, NH, 8, ROWS), f32),
            pltpu.VMEM((NH, NY * ROWS, HEAD), f32),
            pltpu.VMEM((NH, NY * ROWS, HEAD), f32),
            pltpu.VMEM((NH, NY * ROWS, HEAD), f32),
            pltpu.VMEM((ROWS, NH * HEAD), bf16),
            pltpu.VMEM((4, ROWS, COLS), f32),
            pltpu.VMEM((4, 8, ROWS), f32),
            pltpu.VMEM((4, 8, ROWS), f32),
            pltpu.VMEM((2, NP, ROWS, PART), bf16),
            pltpu.VMEM((2, NP, ROWS, PART), bf16),
            pltpu.VMEM((NP, ROWS, PART), bf16),
            pltpu.VMEM((NP, ROWS, PART), bf16),
            pltpu.VMEM((NP, ROWS, PART), f32),
            pltpu.VMEM((ROWS, COLS), f32),
            dma((NG,)),
            dma((NG, 2, 4)),
            dma((NG, NZ + 1)),
            dma((NG, 4)),
            dma((NG, 4)),
            dma((NY,)),
            dma((NY,)),
        ]
        + [dma((NG, NY))] * 4
        + [dma((4,))] * 4
        + [dma((2, NP))] * 2
        + [dma((NP,))] * 2
        + [dma((8,))],
        compiler_params=pltpu.CompilerParams(
            collective_id=0, has_side_effects=True, vmem_limit_bytes=56 * 2**20
        ),
        name="attention_block",
    )(
        query, query_gain, stale_keys, stale_values, hidden, out_weight,
        row(out_bias), row(residual_gate),
    )
    return pl.pallas_call(
        normalise,
        out_shape=(out, out),
        in_specs=[vmem] * 4,
        out_specs=(vmem, vmem),
        compiler_params=pltpu.CompilerParams(vmem_limit_bytes=56 * 2**20),
        name="normalise",
    )(summed, moments, row(norm_shift), row(norm_scale))


def solution(mesh):
    return jax.shard_map(
        body,
        mesh=mesh,
        in_specs=(
            P("patch", None),
            P("patch", "tensor"),
            P("tensor"),
            P("patch", "tensor"),
            P("patch", "tensor"),
            P("tensor", None),
            P(),
            P(),
            P(),
            P(),
        ),
        out_specs=(P("patch", "tensor"), P("patch", "tensor")),
        check_vma=False,
    )
```
